32 devices in a mesh: group: 2 (over x), dp: 16 (over z, y, core).
Axes of the slice: x: 2, y: 2, z: 4, core: 2. Of those that a mesh axis runs over, the one named last changes fastest.
Arguments:
- tokens: bfloat16 [16, 1024, 512], P('dp', 'group'), may hold values from -6 to 6
- qkv_weight: bfloat16 [2, 3, 262144], P(None, None, ('group', 'dp')), may hold values from -0.25 to 0.25
- out_weight: bfloat16 [2, 262144], P(None, ('group', 'dp')), may hold values from -0.75 to 0.75
- ff_weight: bfloat16 [2, 2, 262144], P(None, None, ('group', 'dp')), may hold values from -0.25 to 0.25
- ln_gain: bfloat16 [2, 1024], P(None, ('group', 'dp')), may hold values from 0.5 to 1.5
- ln_bias: bfloat16 [2, 1024], P(None, ('group', 'dp')), may hold values from -2 to 2
- order: int32 [16, 1024], P('dp'), may hold values from 0 to 1023, each once within a row
- cell_lengths: int32 [16, 3], P('dp'), may hold values from 1 to 512, 1024 in all within a row
- known_mask: int32 [16, 512], P('dp'), may hold values 0 or 1
- cotangent: bfloat16 [16, 1024, 512], P('dp', 'group'), may hold values from -6 to 6
Outputs:
- layer_output: float32 [16, 1024, 512], P('dp', 'group')
- input_grad: float32 [16, 1024, 512], P('dp', 'group')
- qkv_grad: float32 [2, 3, 262144], P(None, None, ('group', 'dp'))
- out_proj_grad: float32 [2, 262144], P(None, ('group', 'dp'))
- ff_grad: float32 [2, 2, 262144], P(None, None, ('group', 'dp'))
- gain_grad: float32 [2, 1024], P(None, ('group', 'dp'))
- bias_grad: float32 [2, 1024], P(None, ('group', 'dp'))
The draws below stay inside these ranges and needn't reach their ends.
Inputs may be any that keep to these rules, and one draw needn't show every extreme that they name: Each row of order holds every position of the row once. `cell_lengths`: a row's cell lengths sum to 1024, the longest is exactly 512.
All inputs are finite; a program needn't handle non-finite values. No bound on the sum of `known_mask` on one device may be relied on, other than what follows from the above.
Results may differ from the reference program's by a relative error of at most 0.019.
Values may be sent and summed in bfloat16 or wider, within the bound.
A program may use at most 128 MiB of HBM per device.

```python
import math
import jax
import jax.numpy as jnp
import numpy as np
from jax import lax

D = 512
HEADS = 8
FF = 512
LAYERS = 2
HALF = 512
CELLS = 3
ROWS = 16
ROW_LEN = 1024
MOST = 512


def plant(values, key, low, high):
    dims = values.shape
    place = [jax.random.randint(jax.random.fold_in(key, axis), (), 0, dims[axis]) for axis in range(len(dims))]
    values = values.at[tuple(place)].set(low)
    longest = dims.index(max(dims))
    place[longest] = (place[longest] + 1) % dims[longest]
    return values.at[tuple(place)].set(high)


def steps_of(rng, extent, split, low, largest):
    factor_of, own = 1.0, jax.random.fold_in(rng, 6)
    for dim, blocks in split:
        heights = jnp.exp(jax.random.uniform(jax.random.fold_in(own, dim), (blocks,), jnp.float32, low / len(split), largest / len(split)))
        factor_of = factor_of * jnp.repeat(heights, extent[dim] // blocks).reshape([-1 if axis == dim else 1 for axis in range(len(extent))])
    return factor_of


def profile(amount, total, bound, lean):
    portions = [(1 << 20) // math.isqrt(standing ** lean) + 1 for standing in range(2, amount + 1)]
    surplus, counts = total - bound - (amount - 1), [1] * (amount - 1)
    while surplus > 0:
        movable = [i for i in range(amount - 1) if counts[i] < bound]
        pool, budget = sum([portions[i] for i in movable]), surplus
        for i in movable:
            more = min(bound - counts[i], max(1, budget * portions[i] // pool), surplus)
            counts[i] = counts[i] + more
            surplus = surplus - more
    return np.array([bound] + counts)


def ragged(own_key, count, total, bound, skew):
    if count == 2:
        one = jax.random.randint(own_key, (), max(1, total - bound), min(bound, total - 1) + 1)
        return jnp.stack([one, total - one])
    tallies = jnp.asarray(profile(count, total, bound, skew), jnp.int32)
    couples = (count - 1) // 2
    donor, receiver = tallies[1:1 + 2 * couples:2], tallies[2:2 + 2 * couples:2]
    slack = jnp.minimum(donor - 1, bound - receiver)
    passed = jax.random.randint(jax.random.fold_in(own_key, 1), (couples,), 0, 1 << 20) % (slack + 1)
    tallies = tallies.at[1:1 + 2 * couples:2].set(donor - passed).at[2:2 + 2 * couples:2].set(receiver + passed)
    return tallies[jax.random.permutation(jax.random.fold_in(own_key, 2), count)]


def scatter_about(rng, shape, width, limit, shards=(), kind=jnp.bfloat16):
    entries = width * jax.random.normal(rng, shape, jnp.float32)
    if shards:
        entries = entries * steps_of(rng, shape, shards, -0.22, 0.18)
    return jnp.clip(entries, -limit, limit).astype(kind)


def setup_inputs(seed: int = 0) -> dict:
    streams_of = jax.random.split(jax.random.key(seed), 11)
    tokens = scatter_about(streams_of[0], (ROWS, ROW_LEN, D), 1.0, 6.0, ((0, 16), (1, 2)))
    qkv_weight = scatter_about(streams_of[1], (LAYERS, 3, D * D), D ** -0.5, 0.25, ((2, 32),))
    out_weight = scatter_about(streams_of[2], (LAYERS, D * D), (D // 8) ** -0.5, 0.75, ((1, 32),))
    ff_weight = scatter_about(streams_of[3], (LAYERS, 2, D * FF), D ** -0.5, 0.25, ((2, 32),))
    ln_gain = jnp.clip(1.0 + 0.1 * jax.random.normal(streams_of[4], (LAYERS, 2 * D), jnp.float32), 0.5, 1.5).astype(jnp.bfloat16)
    ln_bias = scatter_about(streams_of[5], (LAYERS, 2 * D), 0.3, 2.0, ((1, 32),))
    order = jax.vmap(lambda own: jax.random.permutation(own, ROW_LEN))(jax.random.split(streams_of[6], ROWS)).reshape((ROWS, ROW_LEN)).astype(jnp.int32)
    cell_lengths = jax.vmap(lambda own: ragged(own, CELLS, ROW_LEN, MOST, 0))(jax.random.split(streams_of[7], ROWS)).reshape((ROWS, CELLS)).astype(jnp.int32)
    known_mask = plant((jax.random.randint(streams_of[8], (ROWS, HALF), 0, 4) < 3).astype(jnp.int32), jax.random.fold_in(streams_of[8], 1), 0, 1)
    cotangent = scatter_about(streams_of[9], (ROWS, ROW_LEN, D), 1.0, 6.0, ((0, 16), (1, 2)))
    return {"tokens": tokens, "qkv_weight": qkv_weight, "out_weight": out_weight, "ff_weight": ff_weight, "ln_gain": ln_gain, "ln_bias": ln_bias, "order": order, "cell_lengths": cell_lengths, "known_mask": known_mask, "cotangent": cotangent}


@jax.custom_vjp
def low(v):
    return lax.optimization_barrier(v.astype(jnp.bfloat16)).astype(jnp.float32)

@jax.custom_vjp
def low_back(v):
    return v

def low_keep(v):
    return (low(v), None)

def low_pass(kept, grad):
    return (grad,)

def back_keep(v):
    return (v, None)

def back_low(kept, grad):
    return (low(grad),)
low.defvjp(low_keep, low_pass)
low_back.defvjp(back_keep, back_low)

def layer_norm(values, gain_vec, bias_vec):
    center = values - lax.optimization_barrier(jnp.mean(values, axis=-1, keepdims=True))
    spread = lax.optimization_barrier(jnp.mean(center * center, axis=-1, keepdims=True))
    return center * lax.rsqrt(spread + 1e-05) * gain_vec + bias_vec

def matmul(left, right):
    return jnp.dot(left, right, precision=lax.Precision.HIGHEST, preferred_element_type=jnp.float32)

def one_row(current, cell_row, mask_row, qkv_all, out_all, ff_all, gain_all, bias_all):
    length = current.shape[0]
    half_len = length // 2
    model_width = current.shape[1]
    head_dim = model_width // HEADS
    score_scale = 1.0 / math.sqrt(head_dim)
    allow = (cell_row[:, None] == cell_row[None, :half_len]) & (mask_row[None, :] == 1)
    allow = allow & (jnp.arange(length)[:, None] != jnp.arange(half_len)[None, :])
    highest = lax.Precision.HIGHEST
    for layer_index in range(LAYERS):
        qkv = qkv_all[layer_index].reshape(3, model_width, model_width)
        w_out = out_all[layer_index].reshape(model_width, model_width)
        w_up = ff_all[layer_index, 0].reshape(model_width, FF)
        w_down = ff_all[layer_index, 1].reshape(FF, model_width)
        gain_one = gain_all[layer_index, :model_width]
        gain_two = gain_all[layer_index, model_width:]
        bias_one = bias_all[layer_index, :model_width]
        bias_two = bias_all[layer_index, model_width:]
        lowered = low(current)
        query = low_back(low(matmul(lowered, qkv[0]))).reshape(length, HEADS, head_dim)
        key_all = low_back(low(matmul(lowered, qkv[1]))).reshape(length, HEADS, head_dim)
        value_all = low_back(low(matmul(lowered, qkv[2]))).reshape(length, HEADS, head_dim)
        known_key = key_all[:half_len]
        known_value = value_all[:half_len]
        scores = low_back(score_scale * jnp.einsum('qhd,khd->hqk', query, known_key, precision=highest))
        scores = jnp.where(allow[None], scores, -1e+30)
        own_score = low_back(score_scale * jnp.einsum('qhd,qhd->hq', query, key_all, precision=highest))
        probs = jax.nn.softmax(jnp.concatenate([scores, own_score[:, :, None]], axis=2), axis=2)
        key_prob = low(probs[:, :, :half_len])
        own_prob = low(probs[:, :, half_len])
        context = jnp.einsum('hqk,khd->qhd', key_prob, known_value, precision=highest)
        context = context + own_prob.T[:, :, None] * value_all
        context = low_back(low(context.reshape(length, model_width)))
        branch = low_back(matmul(context, w_out))
        normed = layer_norm(current + branch, gain_one, bias_one)
        pre_act = low_back(matmul(low(normed), w_up))
        ff_out = low_back(matmul(low(jax.nn.gelu(pre_act)), w_down))
        current = layer_norm(normed + ff_out, gain_two, bias_two)
    return current

def reference(tokens, qkv_weight, out_weight, ff_weight, ln_gain, ln_bias, order, cell_lengths, known_mask, cotangent):
    boundaries = jnp.cumsum(cell_lengths, axis=1)
    cell_of = lax.optimization_barrier(jnp.sum((boundaries[:, None, :] <= order[:, :, None]).astype(jnp.int32), axis=2)).astype(jnp.int32)
    params = (qkv_weight.astype(jnp.float32), out_weight.astype(jnp.float32), ff_weight.astype(jnp.float32), ln_gain.astype(jnp.float32), ln_bias.astype(jnp.float32))

    def row_step(sums_so_far, row_data):
        row_tokens, cell_row, mask_row, row_cot = row_data

        def forward(current, qkv_all, out_all, ff_all, gain_all, bias_all):
            return one_row(current, cell_row, mask_row, qkv_all, out_all, ff_all, gain_all, bias_all)
        result, pullback = jax.vjp(forward, row_tokens.astype(jnp.float32), *params)
        gradients = pullback(row_cot.astype(jnp.float32))
        sums_so_far = tuple((running + addend for running, addend in zip(sums_so_far, gradients[1:])))
        return (sums_so_far, (result, gradients[0]))
    start_sums = tuple((jnp.zeros(param.shape, jnp.float32) for param in params))
    sums, (results, input_grad) = lax.scan(row_step, start_sums, (tokens, cell_of, known_mask, cotangent))
    return (results, input_grad, sums[0], sums[1], sums[2], sums[3], sums[4])
```

```python
import functools
import math

import jax
import jax.numpy as jnp
from jax import lax
from jax.experimental import pallas as pl
from jax.experimental.pallas import tpu as pltpu
from jax.sharding import PartitionSpec as P

HEADS = 8
BLOCKS = 32
ZS = 4
MESH = pl.DeviceIdType.MESH
F32 = jnp.float32
BF16 = jnp.bfloat16

KEY, VALUE, QUERY, OUT, UP, DOWN = range(6)
VECTORS = 6
MATRICES = 13
GATHERS = ((0, 1), (1, 2), (2, 3), (3, 7), (7, 10), (10, 13))
REDUCES = ((9, 12), (6, 9), (3, 6), (0, 3))


def dot(left, right, left_dim, right_dim):
    return lax.dot_general(
        left, right, (((left_dim,), (right_dim,)), ((), ())), preferred_element_type=F32
    )


def kernel(replicas, *refs):
    (
        tok_ref, cot_ref, shard_ref, order_ref, length_ref, known_ref,
        out_ref, inp_ref, grad_ref, vec_ref,
        w, x_in, cot, meta_own, meta, bias, cur, low, qs, ks, vs, kk, kv, probs, own_p,
        ctx, xhat1, r1, normed_low, pre, hidden, xhat2, r2, work, dctx, dq, dkk, dvv,
        send_k, send_v, got_k, got_v,
        g_buf, rc, r2a, r2b, r3, r4, vec_sum, vec_got,
        swap_s, swap_r, ag_s, ag_r, kv_s, kv_r, dkv_s, dkv_r, rs_s, rs_r, vs_s, vs_r,
    ) = refs
    n, d = tok_ref.shape
    hd = d // HEADS
    pairs = d // 128
    scale = 1.0 / math.sqrt(hd)
    gi = lax.axis_index("group")
    dp = lax.axis_index("dp")
    hi, lo = dp // replicas, dp % replicas
    z, y, c = hi // 4, (hi // 2) % 2, hi % 2
    half = dp % 2

    def place(g_, z_, y_, c_):
        return (g_, (z_ * 4 + y_ * 2 + c_) * replicas + lo)

    other_x = place(1 - gi, z, y, c)
    other_y = place(gi, z, 1 - y, c)
    other_c = place(gi, z, y, 1 - c)
    others_z = [place(gi, (z + i) % ZS, y, c) for i in range(1, ZS)]
    sibling = (gi, dp + 1 - 2 * half)
    partner = (1 - gi, dp + 1 - 2 * half)
    is_known = half == 0
    swaps = gi != half

    partners = [other_x, other_y, other_c, partner] + others_z
    if replicas > 1:
        partners.append(sibling)
    barrier = pltpu.get_barrier_semaphore()
    for device in partners:
        pl.semaphore_signal(barrier, inc=1, device_id=device, device_id_type=MESH)

    def remote(src, dst, send, recv, device):
        return pltpu.make_async_remote_copy(
            src_ref=src, dst_ref=dst, send_sem=send, recv_sem=recv, device_id=device, device_id_type=MESH
        )

    def ag_copies(s, phase):
        a, b = GATHERS[s]
        m = pl.ds(a, b - a)
        if phase == 0:
            block = w.at[m, gi, z, y, c]
            plan = [(block, dev) for dev in others_z]
            base = 0
        elif phase == 1:
            plan = [
                (w.at[m, gi, :, y, c, :, pl.ds(0, d // 2)], other_x),
                (w.at[m, gi, :, y, c, :, pl.ds(d // 2, d // 2)], other_y),
            ]
            base = 3
        elif phase == 2:
            plan = [
                (w.at[m, :, :, y, c, :, pl.ds(0, d // 2)], other_y),
                (w.at[m, gi, :, :, c, :, pl.ds(d // 2, d // 2)], other_x),
            ]
            base = 5
        else:
            plan = [(w.at[m, :, :, :, c], other_c)]
            base = 7
        return [remote(r, r, ag_s.at[s, base + i], ag_r.at[s, base + i], dev) for i, (r, dev) in enumerate(plan)]

    def ag_start(s, phase):
        for copy in ag_copies(s, phase):
            copy.start()

    def ag_wait(s, phase):
        for copy in ag_copies(s, phase):
            copy.wait()

    def ag_step(s, phase):
        ag_wait(s, phase - 1)
        ag_start(s, phase)

    def rs_copies(s, phase):
        a, b = REDUCES[s]
        m = pl.ds(a, b - a)
        h0, h1 = pl.ds(0, d // 2), pl.ds(d // 2, d // 2)
        if phase == 0:
            plan = [(g_buf.at[m, :, :, :, 1 - c], rc.at[m], other_c)]
            base = 0
        elif phase == 1:
            plan = [
                (rc.at[m, :, :, 1 - y, :, h0], r2a.at[m], other_y),
                (rc.at[m, 1 - gi, :, :, :, h1], r2b.at[m], other_x),
            ]
            base = 1
        elif phase == 2:
            plan = [
                (r2a.at[m, 1 - gi], r3.at[m, :, :, h0], other_x),
                (r2b.at[m, :, 1 - y], r3.at[m, :, :, h1], other_y),
            ]
            base = 3
        else:
            plan = [(r3.at[m, (z + i) % ZS], r4.at[i - 1, m], others_z[i - 1]) for i in range(1, ZS)]
            base = 5
        return [remote(a_, b_, rs_s.at[s, base + i], rs_r.at[s, base + i], dev) for i, (a_, b_, dev) in enumerate(plan)]

    def rs_start(s, phase):
        for copy in rs_copies(s, phase):
            copy.start()

    def rs_wait(s, phase):
        for copy in rs_copies(s, phase):
            copy.wait()

    def rs_add(s, phase):
        a, b = REDUCES[s]
        h0, h1 = slice(0, d // 2), slice(d // 2, d)
        for m in range(a, b):
            if phase == 0:
                rc[m] = (rc[m].astype(F32) + g_buf[m, :, :, :, c].astype(F32)).astype(BF16)
            elif phase == 1:
                r2a[m] = (r2a[m].astype(F32) + rc[m, :, :, y, :, h0].astype(F32)).astype(BF16)
                r2b[m] = (r2b[m].astype(F32) + rc[m, gi, :, :, :, h1].astype(F32)).astype(BF16)
            elif phase == 2:
                r3[m, :, :, h0] = (r3[m, :, :, h0].astype(F32) + r2a[m, gi].astype(F32)).astype(BF16)
                r3[m, :, :, h1] = (r3[m, :, :, h1].astype(F32) + r2b[m, :, y].astype(F32)).astype(BF16)
            else:
                total = r3[m, z].astype(F32)
                for i in range(ZS - 1):
                    total = total + r4[i, m].astype(F32)
                grad_ref[m] = total

    def rs_step(s, phase):
        rs_wait(s, phase - 1)
        rs_add(s, phase - 1)
        if phase < 4:
            rs_start(s, phase)

    def vec_copies(phase):
        if phase == 3:
            return [
                remote(vec_sum.at[3], vec_got.at[2 + i], vs_s.at[2 + i], vs_r.at[2 + i], others_z[i - 1])
                for i in range(1, ZS)
            ]
        device = (other_c, other_y, other_x)[phase]
        return [remote(vec_sum.at[phase], vec_got.at[phase], vs_s.at[phase], vs_r.at[phase], device)]

    def vec_start(phase):
        for copy in vec_copies(phase):
            copy.start()

    def vec_step(phase):
        for copy in vec_copies(phase - 1):
            copy.wait()
        if phase < 4:
            vec_sum[phase] = vec_sum[phase - 1] + vec_got[phase - 1]
            vec_start(phase)

    def swap_copy(index, src, dst):
        return remote(src, dst, swap_s.at[index], swap_r.at[index], partner)

    w[:, gi, z, y, c] = shard_ref[...]
    position = order_ref[...]
    cell = jnp.zeros(position.shape, jnp.int32)
    edge = jnp.zeros((1, 1), jnp.int32)
    for i in range(length_ref.shape[1]):
        edge = edge + length_ref[:, i : i + 1]
        cell = cell + (edge <= position).astype(jnp.int32)
    meta_own[0:1, :] = cell.astype(F32)
    meta_own[1:2, 0:n] = known_ref[...].astype(F32)

    pl.semaphore_wait(barrier, len(partners))
    for s in range(4):
        ag_start(s, 0)

    @pl.when(swaps)
    def _():
        swap_copy(0, meta_own, meta).start()
        swap_copy(1, tok_ref, x_in).start()

    @pl.when(jnp.logical_not(swaps))
    def _():
        meta[...] = meta_own[...]
        x_in[...] = tok_ref[...]
        cot[...] = cot_ref[...]

    ag_step(0, 1)
    ag_step(1, 1)
    ag_step(0, 2)
    ag_step(2, 1)
    ag_step(1, 2)
    ag_step(0, 3)

    lane = lax.broadcasted_iota(jnp.int32, (HEADS, d), 1)
    head_of = (lane // hd == lax.broadcasted_iota(jnp.int32, (HEADS, d), 0)).astype(BF16)

    def head_sum(product):
        high = product.astype(BF16)
        rest = (product - high.astype(F32)).astype(BF16)
        return dot(head_of, high, 1, 1) + dot(head_of, rest, 1, 1)

    def weight(i):
        return w[i].reshape(d, d)

    @pl.when(swaps)
    def _():
        swap_copy(0, meta_own, meta).wait()

    kinds = lax.broadcasted_iota(jnp.int32, (HEADS, n), 0).astype(F32)
    query_cell = jnp.where(is_known, meta[0:1, 0:n], meta[0:1, n : 2 * n])
    query_code = (kinds == query_cell).astype(BF16)
    key_code = ((kinds == meta[0:1, 0:n]) & (meta[1:2, 0:n] == 1.0)).astype(BF16)
    same = dot(key_code, query_code, 0, 0)
    key_at = lax.broadcasted_iota(jnp.int32, (n, n), 0)
    query_at = lax.broadcasted_iota(jnp.int32, (n, n), 1) + half * 2 * n
    bias[...] = jnp.where((same > 0.5) & (key_at != query_at), 0.0, -1e30)

    ag_step(2, 2)
    ag_step(1, 3)
    ag_step(3, 1)
    ag_step(2, 3)

    @pl.when(swaps)
    def _():
        swap_copy(1, tok_ref, x_in).wait()
        swap_copy(2, cot_ref, cot).start()

    cur[...] = x_in[...].astype(F32)

    def in_head(h, value):
        at = lax.broadcasted_iota(jnp.int32, value.shape, 1)
        return jnp.where(at // hd == h, value, jnp.zeros_like(value))

    def pair_lanes(i):
        return pl.ds(pl.multiple_of(i * 128, 128), 128)

    def kv_copies(l):
        return [
            remote(kk.at[l], kk.at[l], kv_s.at[l, 0], kv_r.at[l, 0], sibling),
            remote(kv.at[l], kv.at[l], kv_s.at[l, 1], kv_r.at[l, 1], sibling),
        ]

    def attend(l, first, last):
        def body(i, carry):
            lanes = pair_lanes(i)
            k_pair, v_pair, q_pair = kk[l, :, lanes], kv[l, :, lanes], qs[l, :, lanes]
            total_ctx = jnp.zeros((n, 128), F32)
            for h in range(2):
                own = own_p[l, pl.ds(i * 2 + h, 1), :]
                scores = dot(in_head(h, k_pair), q_pair, 1, 1) + bias[...]
                top = jnp.maximum(jnp.max(scores, axis=0, keepdims=True), own)
                weights = jnp.exp(scores - top)
                own_weight = jnp.exp(own - top)
                inverse = 1.0 / (jnp.sum(weights, axis=0, keepdims=True) + own_weight)
                prob = (weights * inverse).astype(BF16)
                probs[l, i * 2 + h] = prob
                own_p[l, pl.ds(i * 2 + h, 1), :] = (own_weight * inverse).astype(BF16).astype(F32)
                total_ctx = total_ctx + dot(prob, in_head(h, v_pair), 0, 0)
            work[:, lanes] = total_ctx
            return carry

        lax.fori_loop(first, last, body, 0)

    def norm(values, gain, shift, xhat, spread):
        center = values - jnp.mean(values, axis=1, keepdims=True)
        r = lax.rsqrt(jnp.mean(center * center, axis=1, keepdims=True) + 1e-05)
        hat = center * r
        xhat[...] = hat.astype(BF16)
        spread[...] = r
        return hat * gain + shift

    def vectors(l):
        blocks = w[VECTORS, :, :, :, :, :, 0:128].reshape(BLOCKS, 16, 128)
        rows = jnp.sum(blocks.astype(F32), axis=1).astype(BF16)
        wide = 2 * d
        per = wide // BLOCKS
        source = lax.broadcasted_iota(jnp.int32, (128, wide), 0)
        target = lax.broadcasted_iota(jnp.int32, (128, wide), 1)
        owner = lax.broadcasted_iota(jnp.int32, (BLOCKS, wide), 0)
        column = lax.broadcasted_iota(jnp.int32, (BLOCKS, wide), 1)
        found = []
        for which in range(2):
            pick = (source == target % per + (l * 2 + which) * per).astype(BF16)
            spread_out = dot(rows, pick, 1, 0)
            found.append(jnp.sum(jnp.where(column // per == owner, spread_out, 0.0), axis=0, keepdims=True))
        gains, shifts = found
        return gains[:, :d], shifts[:, :d], gains[:, d:], shifts[:, d:]

    def forward(l, first_point, mid_point, late_point, chunks):
        base = l * 7
        low[l] = cur[...].astype(BF16)
        if chunks[0] is not None:
            ag_wait(chunks[0], 3)
        ks[l] = dot(low[l], weight(base + KEY), 1, 0).astype(BF16)

        @pl.when(is_known)
        def _():
            kk[l] = ks[l]
            kv_copies(l)[0].start()

        if chunks[1] is not None:
            ag_wait(chunks[1], 3)
        vs[l] = dot(low[l], weight(base + VALUE), 1, 0).astype(BF16)

        @pl.when(is_known)
        def _():
            kv[l] = vs[l]
            kv_copies(l)[1].start()

        if chunks[2] is not None:
            ag_wait(chunks[2], 3)
        qs[l] = (dot(low[l], weight(base + QUERY), 1, 0).astype(BF16).astype(F32) * scale).astype(BF16)
        own_p[l] = head_sum(qs[l].astype(F32) * ks[l].astype(F32))
        first_point()

        @pl.when(jnp.logical_not(is_known))
        def _():
            for copy in kv_copies(l):
                copy.wait_recv()

        attend(l, 0, pairs // 2)
        mid_point()
        attend(l, pairs // 2, pairs)
        spread_own = dot(own_p[l].astype(BF16), head_of, 0, 0)
        ctx[l] = (work[...] + spread_own * vs[l].astype(F32)).astype(BF16)
        late_point()
        gain1, shift1, gain2, shift2 = vectors(l)
        first_in = cur[...] + dot(ctx[l], weight(base + OUT), 1, 0)
        normed = norm(first_in, gain1, shift1, xhat1.at[l], r1.at[l])
        work[...] = normed
        normed_low[l] = normed.astype(BF16)
        pre_act = dot(normed_low[l], weight(base + UP), 1, 0)
        pre[l] = pre_act
        hidden[l] = jax.nn.gelu(pre_act).astype(BF16)
        second_in = work[...] + dot(hidden[l], weight(base + DOWN), 1, 0)
        cur[...] = norm(second_in, gain2, shift2, xhat2.at[l], r2.at[l])

    def first0():
        ag_step(3, 2)
        ag_start(4, 0)
        ag_start(5, 0)

    def mid0():
        ag_step(3, 3)
        ag_step(4, 1)
        ag_step(5, 1)

    def late0():
        ag_wait(3, 3)
        ag_step(4, 2)
        ag_step(5, 2)

    forward(0, first0, mid0, late0, (0, 1, 2))
    ag_step(4, 3)
    ag_wait(4, 3)

    def mid1():
        ag_step(5, 3)

    def late1():
        ag_wait(5, 3)

    forward(1, lambda: None, mid1, late1, (None, None, None))
    x_in[...] = cur[...].astype(BF16)

    @pl.when(swaps)
    def _():
        swap_copy(3, x_in, out_ref).start()
        swap_copy(2, cot_ref, cot).wait()

    @pl.when(jnp.logical_not(swaps))
    def _():
        out_ref[...] = x_in[...]

    cur[...] = cot[...].astype(F32)

    def norm_back(grad, gain, xhat, spread):
        hat = xhat[...].astype(F32)
        e = grad * gain
        mean_e = jnp.mean(e, axis=1, keepdims=True)
        mean_eh = jnp.mean(e * hat, axis=1, keepdims=True)
        out = spread[...] * (e - mean_e - hat * mean_eh)
        return out, jnp.sum(grad * hat, axis=0, keepdims=True), jnp.sum(grad, axis=0, keepdims=True)

    def dkv_copies(l, i):
        lanes = pair_lanes(i)
        return [
            remote(send_k.at[l, :, lanes], got_k.at[l, :, lanes], dkv_s.at[l, i, 0], dkv_r.at[l, i, 0], sibling),
            remote(send_v.at[l, :, lanes], got_v.at[l, :, lanes], dkv_s.at[l, i, 1], dkv_r.at[l, i, 1], sibling),
        ]

    def store_grad(index, value):
        g_buf[index] = value.astype(BF16).reshape(g_buf.shape[1:])

    def backward(l, start_point, ff_point, attn_point, mid_point, end_point):
        base, gbase = l * 7, l * 6
        gain1, shift1, gain2, shift2 = vectors(l)
        grad_second, grad_gain2, grad_shift2 = norm_back(cur[...], gain2, xhat2.at[l], r2.at[l])
        work[...] = grad_second
        grad_ff = grad_second.astype(BF16)
        store_grad(gbase + DOWN, dot(hidden[l], grad_ff, 0, 0))
        start_point()
        grad_hidden = dot(grad_ff, weight(base + DOWN), 1, 1)
        act = pre[l]
        coef = math.sqrt(2.0 / math.pi)
        tanh = jnp.tanh(coef * (act + 0.044715 * act * act * act))
        slope = 0.5 * (1.0 + tanh) + 0.5 * act * (1.0 - tanh * tanh) * coef * (1.0 + 3 * 0.044715 * act * act)
        grad_pre = (grad_hidden * slope).astype(BF16)
        store_grad(gbase + UP, dot(normed_low[l], grad_pre, 0, 0))
        grad_normed = work[...] + dot(grad_pre, weight(base + UP), 1, 1)
        ff_point()
        grad_first, grad_gain1, grad_shift1 = norm_back(grad_normed, gain1, xhat1.at[l], r1.at[l])
        cur[...] = grad_first
        grad_branch = grad_first.astype(BF16)
        vec_sum[0, l * 4 : l * 4 + 1, 0:d] = grad_gain1
        vec_sum[0, l * 4 : l * 4 + 1, d : 2 * d] = grad_gain2
        vec_sum[0, l * 4 + 1 : l * 4 + 2, 0:d] = grad_shift1
        vec_sum[0, l * 4 + 1 : l * 4 + 2, d : 2 * d] = grad_shift2
        store_grad(gbase + OUT, dot(ctx[l], grad_branch, 0, 0))
        dctx[...] = dot(grad_branch, weight(base + OUT), 1, 1).astype(BF16)
        wide_grad = dctx[...].astype(F32)
        delta = head_sum(wide_grad * ctx[l].astype(F32))
        own_grad = head_sum(wide_grad * vs[l].astype(F32))
        own_score_grad = (own_p[l] * (own_grad - delta)).astype(BF16)
        work[0:HEADS, :] = delta
        attn_point()

        def body(i, carry):
            lanes = pair_lanes(i)
            k_pair, v_pair, q_pair = kk[l, :, lanes], kv[l, :, lanes], qs[l, :, lanes]
            c_pair = dctx[:, lanes]
            sum_q = jnp.zeros((n, 128), F32)
            sum_k = jnp.zeros((n, 128), F32)
            sum_v = jnp.zeros((n, 128), F32)
            for h in range(2):
                prob = probs[l, i * 2 + h]
                grad_prob = dot(in_head(h, v_pair), c_pair, 1, 1)
                shift = work[pl.ds(i * 2 + h, 1), :]
                grad_score = (prob.astype(F32) * (grad_prob - shift)).astype(BF16)
                sum_v = sum_v + dot(prob, in_head(h, c_pair), 1, 0)
                sum_k = sum_k + dot(grad_score, in_head(h, q_pair), 1, 0)
                sum_q = sum_q + dot(grad_score, in_head(h, k_pair), 0, 0)
            dq[:, lanes] = sum_q

            @pl.when(is_known)
            def _():
                dkk[:, lanes] = sum_k
                dvv[:, lanes] = sum_v

            @pl.when(jnp.logical_not(is_known))
            def _():
                send_k[l, :, lanes] = sum_k.astype(BF16)
                send_v[l, :, lanes] = sum_v.astype(BF16)
                for copy in dkv_copies(l, i):
                    copy.start()

            return carry

        lax.fori_loop(0, pairs // 2, body, 0)
        mid_point()
        lax.fori_loop(pairs // 2, pairs, body, 0)
        own_wide = dot(own_score_grad, head_of, 0, 0)
        p_wide = dot(own_p[l].astype(BF16), head_of, 0, 0)
        query_grad = (scale * (dq[...] + own_wide * ks[l].astype(F32))).astype(BF16)
        store_grad(gbase + QUERY, dot(low[l], query_grad, 0, 0))
        cur[...] += dot(query_grad, weight(base + QUERY), 1, 1)
        own_k = own_wide * qs[l].astype(F32)
        own_v = p_wide * dctx[...].astype(F32)

        @pl.when(is_known)
        def _():
            for i in range(pairs):
                for copy in dkv_copies(l, i):
                    copy.wait_recv()
            dkk[...] = dkk[...] + got_k[l].astype(F32) + own_k
            dvv[...] = dvv[...] + got_v[l].astype(F32) + own_v

        @pl.when(jnp.logical_not(is_known))
        def _():
            dkk[...] = own_k
            dvv[...] = own_v

        key_grad = dkk[...].astype(BF16)
        value_grad = dvv[...].astype(BF16)
        store_grad(gbase + KEY, dot(low[l], key_grad, 0, 0))
        store_grad(gbase + VALUE, dot(low[l], value_grad, 0, 0))
        end_point()
        cur[...] += dot(key_grad, weight(base + KEY), 1, 1) + dot(value_grad, weight(base + VALUE), 1, 1)

    vec_sum[0] = jnp.zeros(vec_sum.shape[1:], F32)

    backward(1, lambda: None, lambda: None, lambda: rs_start(0, 0), lambda: rs_step(0, 1), lambda: rs_start(1, 0))

    def start0():
        rs_step(0, 2)
        rs_step(1, 1)

    def ff0():
        rs_step(0, 3)

    def attn0():
        rs_step(1, 2)
        rs_start(2, 0)
        vec_start(0)

    def mid0b():
        rs_step(0, 4)
        rs_step(1, 3)
        rs_step(2, 1)
        vec_step(1)

    def end0():
        rs_start(3, 0)
        rs_step(2, 2)
        vec_step(2)
        rs_step(1, 4)

    backward(0, start0, ff0, attn0, mid0b, end0)
    cot[...] = cur[...].astype(BF16)

    @pl.when(swaps)
    def _():
        swap_copy(4, cot, inp_ref).start()

    @pl.when(jnp.logical_not(swaps))
    def _():
        inp_ref[...] = cot[...]

    rs_step(3, 1)
    rs_step(2, 3)
    vec_step(3)
    rs_step(3, 2)
    rs_step(3, 3)
    rs_step(2, 4)
    vec_step(4)
    all_sums = vec_sum[3]
    for i in range(ZS - 1):
        all_sums = all_sums + vec_got[3 + i]
    wide = 2 * d
    per = wide // BLOCKS
    me = ((gi * ZS + z) * 2 + y) * 2 + c
    column = lax.broadcasted_iota(jnp.int32, (HEADS, wide), 1)
    mine = jnp.where(column // per == me, all_sums, 0.0)
    source = lax.broadcasted_iota(jnp.int32, (wide, 128), 0)
    target = lax.broadcasted_iota(jnp.int32, (wide, 128), 1)
    fold = (source % per == target).astype(F32)
    vec_ref[...] = lax.dot_general(
        mine, fold, (((1,), (0,)), ((), ())), preferred_element_type=F32, precision=lax.Precision.HIGHEST
    )
    rs_step(3, 4)

    @pl.when(is_known)
    def _():
        for l in range(2):
            for copy in kv_copies(l):
                copy.wait_send()

    @pl.when(jnp.logical_not(is_known))
    def _():
        for l in range(2):
            for i in range(pairs):
                for copy in dkv_copies(l, i):
                    copy.wait_send()

    @pl.when(swaps)
    def _():
        swap_copy(3, x_in, out_ref).wait()
        swap_copy(4, cot, inp_ref).wait()


def run_kernel(tokens, cotangent, blocks, order, lengths, known, replicas):
    n, d = tokens.shape
    layers = 2
    vmem = pl.BlockSpec(memory_space=pltpu.VMEM)

    def buf(*shape, dtype=BF16):
        return pltpu.VMEM(shape, dtype)

    grid = (2, ZS, 2, 2, 16)
    dma = pltpu.SemaphoreType.DMA
    scratch = [
        buf(MATRICES, *grid, d),
        buf(n, d), buf(n, d),
        buf(8, 2 * n, dtype=F32), buf(8, 2 * n, dtype=F32),
        buf(n, n, dtype=F32),
        buf(n, d, dtype=F32),
        buf(layers, n, d), buf(layers, n, d), buf(layers, n, d), buf(layers, n, d),
        buf(layers, n, d), buf(layers, n, d),
        buf(layers, HEADS, n, n),
        buf(layers, HEADS, n, dtype=F32),
        buf(layers, n, d),
        buf(layers, n, d), buf(layers, n, 1, dtype=F32),
        buf(layers, n, d), buf(layers, n, d, dtype=F32), buf(layers, n, d),
        buf(layers, n, d), buf(layers, n, 1, dtype=F32),
        buf(n, d, dtype=F32), buf(n, d),
        buf(n, d, dtype=F32), buf(n, d, dtype=F32), buf(n, d, dtype=F32),
        buf(layers, n, d), buf(layers, n, d), buf(layers, n, d), buf(layers, n, d),
        buf(12, *grid, d),
        buf(12, 2, ZS, 2, 16, d),
        buf(12, 2, ZS, 16, d // 2), buf(12, ZS, 2, 16, d // 2),
        buf(12, ZS, 16, d), buf(ZS - 1, 12, 16, d),
        buf(4, 8, 2 * d, dtype=F32), buf(6, 8, 2 * d, dtype=F32),
        dma((5,)), dma((5,)),
        dma((len(GATHERS), 8)), dma((len(GATHERS), 8)),
        dma((layers, 2)), dma((layers, 2)),
        dma((layers, d // 128, 2)), dma((layers, d // 128, 2)),
        dma((len(REDUCES), 8)), dma((len(REDUCES), 8)),
        dma((6,)), dma((6,)),
    ]
    return pl.pallas_call(
        functools.partial(kernel, replicas),
        out_shape=(
            jax.ShapeDtypeStruct((n, d), BF16),
            jax.ShapeDtypeStruct((n, d), BF16),
            jax.ShapeDtypeStruct((12, 16, d), F32),
            jax.ShapeDtypeStruct((8, 128), F32),
        ),
        in_specs=[vmem] * 6,
        out_specs=(vmem,) * 4,
        scratch_shapes=scratch,
        compiler_params=pltpu.CompilerParams(
            collective_id=0, has_side_effects=True, vmem_limit_bytes=62 * 2**20
        ),
    )(tokens, cotangent, blocks, order, lengths, known)


def shards(
    tokens, qkv_weight, out_weight, ff_weight, ln_gain, ln_bias, order, cell_lengths, known_mask, cotangent
):
    _, half_len, d = tokens.shape
    dp_size = lax.axis_size("dp")
    replicas = dp_size * 2 // BLOCKS
    groups = [[i * replicas + j for j in range(replicas)] for i in range(dp_size // replicas)]
    rows = d // (2 * dp_size)

    def square(array, layer, *which):
        return array[(layer, *which)].reshape(1, rows, d)

    pieces = []
    for layer in range(2):
        pieces += [square(qkv_weight, layer, 1), square(qkv_weight, layer, 2), square(qkv_weight, layer, 0)]
        pieces += [square(out_weight, layer), square(ff_weight, layer, 0), square(ff_weight, layer, 1)]
    mats = jnp.concatenate(pieces, axis=0)
    vecs = jnp.stack([ln_gain[0], ln_bias[0], ln_gain[1], ln_bias[1]])
    if replicas > 1:
        mats = lax.all_gather(mats, "dp", axis=1, tiled=True, axis_index_groups=groups)
        vecs = lax.all_gather(vecs, "dp", axis=1, tiled=True, axis_index_groups=groups)
    vecs = jnp.pad(vecs.reshape(1, 1, -1), ((0, 0), (0, 15), (0, d - vecs.size)))
    blocks = jnp.concatenate([mats[:6], vecs, mats[6:]], axis=0)
    out, inp, grads, vec = run_kernel(
        tokens[0], cotangent[0], blocks, order, cell_lengths, known_mask, replicas
    )
    per = 2 * d // BLOCKS
    vec = vec[:, :per]
    if replicas > 1:
        grads = lax.psum_scatter(grads, "dp", scatter_dimension=1, tiled=True, axis_index_groups=groups)
        vec = lax.psum_scatter(vec, "dp", scatter_dimension=1, tiled=True, axis_index_groups=groups)
    grads = grads.reshape(2, 6, -1)
    qkv_grad = jnp.stack([grads[:, QUERY], grads[:, KEY], grads[:, VALUE]], axis=1)
    ff_grad = grads[:, UP : DOWN + 1]
    return (
        out.astype(F32)[None],
        inp.astype(F32)[None],
        qkv_grad,
        grads[:, OUT],
        ff_grad,
        vec[0::4],
        vec[1::4],
    )


def solution(mesh):
    flat = ("group", "dp")
    return jax.shard_map(
        shards,
        mesh=mesh,
        in_specs=(
            P("dp", "group", None),
            P(None, None, flat),
            P(None, flat),
            P(None, None, flat),
            P(None, flat),
            P(None, flat),
            P("dp", None),
            P("dp", None),
            P("dp", None),
            P("dp", "group", None),
        ),
        out_specs=(
            P("dp", "group", None),
            P("dp", "group", None),
            P(None, None, flat),
            P(None, flat),
            P(None, None, flat),
            P(None, flat),
            P(None, flat),
        ),
        check_vma=False,
    )
```

```python
import functools
import math

import jax
import jax.numpy as jnp
from jax import lax
from jax.experimental import pallas as pl
from jax.experimental.pallas import tpu as pltpu
from jax.sharding import PartitionSpec as P

HEADS = 8
BLOCKS = 32
ZS = 4
MESH = pl.DeviceIdType.MESH
F32 = jnp.float32
BF16 = jnp.bfloat16

KEY, VALUE, QUERY, OUT, UP, DOWN = range(6)
VECTORS = 3
MATRICES = 13
GATHERS = (
    (0, 3, ((0, 128, "z,y,x"),)),
    (0, 3, ((128, 128, "z,x,y"),)),
    (0, 3, ((256, 128, "x,z,y"), (384, 128, "z,y,x"))),
    (3, 4, ((0, 128, "y,x,z"),)),
    (4, 5, ((0, 256, "z,y,x"), (256, 256, "x,y,z"))),
    (5, 6, ((0, 256, "y,z,x"), (256, 256, "z,x,y"))),
    (6, 7, ((0, 256, "z,x,y"), (256, 256, "y,z,x"))),
    (7, 10, ((0, 128, "x,z,y"), (128, 128, "z,y,x"))),
    (7, 10, ((256, 128, "z,y,x"), (384, 128, "z,x,y"))),
    (10, 11, ((0, 256, "x,y,z"), (256, 256, "y,x,z"))),
    (11, 12, ((0, 512, "y,z,x"),)),
    (12, 13, ((0, 256, "x,z,y"), (256, 256, "y,x,z"))),
)
REDUCES = (
    (11, 12, ((0, 256, "y,z,x"), (256, 256, "z,y,x"))),
    (10, 11, ((0, 512, "z,y,x"),)),
    (9, 10, ((0, 256, "y,x,z"), (256, 256, "z,y,x"))),
    (6, 9, ((0, 128, "y,x,z"), (128, 128, "x,y,z"))),
    (6, 9, ((256, 128, "z,y,x"), (384, 128, "y,x,z"))),
    (5, 6, ((0, 256, "y,x,z"), (256, 256, "x,y,z"))),
    (4, 5, ((0, 256, "z,x,y"), (256, 256, "x,y,z"))),
    (3, 4, ((0, 256, "x,y,z"), (256, 256, "z,y,x"))),
    (0, 3, ((0, 128, "x,y,z"), (128, 128, "y,z,x"))),
    (0, 3, ((256, 128, "y,z,x"),)),
    (0, 3, ((384, 128, "y,x,z"),)),
)
SEGMENTS = (((0, 128), (128, 128), (256, 256)), ((0, 256), (256, 256)))
BACK_SEGMENTS = (((0, 256), (256, 128), (384, 128)), ((0, 256), (256, 256)))
NEEDS = {
    "layer 0 need 0": 0, "layer 0 need 1": 1, "layer 0 need 2": 2, "layer 0 context": 4, "layer 0 vectors": 3,
    "layer 0 normed": 5, "layer 0 hidden": 6, "layer 1 need 0": 7, "layer 1 need 1": 8, "layer 1 context": 9,
    "layer 1 normed": 10, "layer 1 hidden": 11,
}
SCHEDULE = {
    "start": ("g2.0", "g1.0", "g0.0", "g6.0", "g4.0", "g5.0", "g3.0", "tokens",),
    "layer 0 need 0": ("g3.1", "g2.1", "g1.1", "g0.1", "g7.0", "g6.1", "g4.1", "g10.0", "g9.0", "g8.0", "g5.1", "g0.2", "g3.2", "g11.0", "g1.2", "g2.2", "g7.1", "g4.2", "g10.1", "g9.1", "g6.2", "g0.3", "g11.1",),
    "layer 0 columns 0": ("g1.3", "g8.1",),
    "layer 0 pair 0": ("g5.2",),
    "layer 0 columns 1": ("g2.3", "g3.3",),
    "layer 0 pair 1": ("g7.2", "g9.2",),
    "layer 0 columns 2": ("g6.3",),
    "layer 0 pair 2": ("g8.2", "g4.3",),
    "layer 0 pair 3": ("g5.3",),
    "layer 0 normed": ("g7.3", "g10.2",),
    "layer 0 done": ("g11.2",),
    "layer 1 columns 0": ("g8.3", "cotangent",),
    "layer 1 columns 1": ("g10.3",),
    "layer 1 pair 2": ("g9.3",),
    "layer 1 context": ("g11.3",),
    "back 1 down": ("r0.0",),
    "back 1 up": ("r1.0",),
    "back 1 out": ("r2.0",),
    "back 1 attend": ("r0.1",),
    "back 1 wide": ("r1.1",),
    "back 1 pair 0": ("r2.1",),
    "back 1 pair 3": ("r0.2",),
    "back 1 key 0": ("r3.0",),
    "back 1 key 1": ("r4.0",),
    "back 0 down": ("r5.0", "r3.1",),
    "back 0 up": ("r4.1", "r1.2", "r6.0",),
    "back 0 out": ("r7.0",),
    "back 0 context": ("r5.1",),
    "back 0 attend": ("vec.0",),
    "back 0 wide": ("r2.2", "r6.1",),
    "back 0 pair 0": ("vec.1", "r0.3", "r3.2", "r7.1",),
    "back 0 pair 2": ("r4.2", "r1.3",),
    "back 0 key 0": ("r8.0", "r5.2", "r0.4",),
    "back 0 query 1": ("r2.3",),
    "back 0 pair 3": ("vec.2", "r3.3", "r6.2",),
    "back 0 key 1": ("r9.0", "r8.1",),
    "back 0 key 2": ("r10.0", "r4.3",),
    "back 0 done": ("result", "r9.1", "vec.3", "r5.3", "r2.4", "r10.1", "r1.4", "r7.2", "r6.3", "r3.4", "r8.2", "r4.4", "vec.4", "r9.2", "r5.4", "r10.2", "r7.3", "r6.4", "r8.3", "r10.3", "r9.3", "r7.4", "r8.4", "r9.4", "r10.4",),
}


def axes_of(parts):
    return parts[0][2].split(",")


def first_semaphores(plan):
    at = [0]
    for _, _, parts in plan:
        at.append(at[-1] + (4 if parts[0][2] == "all" else len(axes_of(parts)) * len(parts)) + 1)
    return at


AT_GATHER = first_semaphores(GATHERS)
AT_REDUCE = first_semaphores(REDUCES)


def place_of(l, index):
    return l * 7 + index + (l == 0 and index >= VECTORS)

def dot(left, right, left_dim, right_dim):
    return lax.dot_general(
        left, right, (((left_dim,), (right_dim,)), ((), ())), preferred_element_type=F32
    )


def kernel(replicas, *refs):
    (
        tok_ref, cot_ref, qkv_ref, outw_ref, ff_ref, gain_ref, shift_ref, order_ref, length_ref, known_ref,
        out_ref, inp_ref, grad_ref, vec_ref,
        w, x_in, cot, meta_own, meta, query_code, key_code, found_self, cur, low, qs, ks, vs, kkv, probs, own_e, inverses,
        ctx, xhat1, r1, normed_low, pre, hidden, xhat2, r2, work, dctx, dq, dkk, dvv, shifts, dqb, dkb, dvb,
        send_kv, got_kv,
        g_buf, rc, rx, vec_sum, vec_got,
        swap_s, swap_r, ag_s, ag_r, kv_s, kv_r, dkv_s, dkv_r, rs_s, rs_r, vs_s, vs_r,
    ) = refs
    n, d = tok_ref.shape
    hd = d // HEADS
    pairs = d // 128
    scale = 1.0 / math.sqrt(hd)
    gi = lax.axis_index("group")
    dp = lax.axis_index("dp")
    hi, lo = dp // replicas, dp % replicas
    z, y, c = hi // 4, (hi // 2) % 2, hi % 2
    half = dp % 2

    def place(g_, z_, y_, c_):
        return (g_, (z_ * 4 + y_ * 2 + c_) * replicas + lo)

    other_x = place(1 - gi, z, y, c)
    other_y = place(gi, z, 1 - y, c)
    other_c = place(gi, z, y, 1 - c)
    others_z = [place(gi, (z + i) % ZS, y, c) for i in range(1, ZS)]
    targets = {"x": [other_x], "y": [other_y], "z": others_z}
    apart = [
        (dx, dy, [(dz, place((gi + dx) % 2, (z + dz) % ZS, (y + dy) % 2, c)) for dz in range(dx + dy == 0, ZS)])
        for dx in range(2)
        for dy in range(2)
    ]
    sibling = (gi, dp + 1 - 2 * half)
    partner = (1 - gi, dp + 1 - 2 * half)
    is_known = half == 0
    swaps = gi != half

    partners = [other_c, partner] + [device for _, _, steps in apart for _, device in steps]
    if replicas > 1:
        partners.append(sibling)
    barrier = pltpu.get_barrier_semaphore()
    for device in partners:
        pl.semaphore_signal(barrier, inc=1, device_id=device, device_id_type=MESH)

    def remote(src, dst, send, recv, device):
        return pltpu.make_async_remote_copy(
            src_ref=src, dst_ref=dst, send_sem=send, recv_sem=recv, device_id=device, device_id_type=MESH
        )

    def ag_copies(s, phase):
        a, b, parts = GATHERS[s]
        m = pl.ds(a, b - a)
        copies, waits = [], []

        def add(block, three, devices, k):
            at = AT_GATHER[s] + k
            copies.extend(remote(block, block, ag_s.at[at], ag_r.at[at], device) for device in devices)
            waits.append(remote(three, three, ag_s.at[at], ag_r.at[at], devices[0]))

        if phase == len(axes_of(parts)):
            cols = pl.ds(parts[0][0], sum(count for _, count, _ in parts))
            block = w.at[m, :, :, :, c, :, cols]
            add(block, block, [other_c], AT_GATHER[s + 1] - AT_GATHER[s] - 1)
            return copies, waits
        if parts[0][2] == "all":
            cols = pl.ds(parts[0][0], parts[0][1])
            block = w.at[m, gi, z, y, c, :, cols]
            for k, (dx, dy, steps) in enumerate(apart):
                arrived = w.at[m, (gi + dx) % 2, pl.ds(0, len(steps)), (y + dy) % 2, c, :, cols]
                add(block, arrived, [device for _, device in steps], k)
            return copies, waits
        for k, (first, count, order) in enumerate(parts):
            axes = order.split(",")
            done = axes[:phase]
            x_at, z_at, y_at = (
                slice(None) if axis in done else own for axis, own in (("x", gi), ("z", z), ("y", y))
            )
            cols = pl.ds(first, count)
            block = w.at[m, x_at, z_at, y_at, c, :, cols]
            three = w.at[m, x_at, pl.ds(0, ZS - 1), y_at, c, :, cols] if axes[phase] == "z" else block
            add(block, three, targets[axes[phase]], phase * len(parts) + k)
        return copies, waits

    def ag_start(s, phase):
        for copy in ag_copies(s, phase)[0]:
            copy.start()

    def ag_wait(s, phase):
        for copy in ag_copies(s, phase)[1]:
            copy.wait()

    def ag_step(s, phase):
        if phase:
            ag_wait(s, phase - 1)
        ag_start(s, phase)

    def ag_finish(s):
        ag_wait(s, len(axes_of(GATHERS[s][2])))

    def rs_plan(s, phase):
        a, b, parts = REDUCES[s]
        m = slice(a, b)
        plan = []
        for first, count, order in parts:
            axes = order.split(",")
            cols = slice(first, first + count)
            axis, before = axes[phase - 1], axes[: phase - 1]

            def pick(value, after):
                where = (value if one == axis else (after[one] if one in before else slice(None)) for one in "xzy")
                return (m, *where, slice(None), cols)

            own = {"x": gi, "y": y, "z": z}
            spent = {"x": 1, "y": 1, "z": ZS - 1}
            if axis == "z":
                sends = [(pick((z + i) % ZS, own), pick(i - 1, spent)) for i in range(1, ZS)]
                arrived = [pick(i, spent) for i in range(ZS - 1)]
                both = pick(slice(0, ZS - 1), own), pick(slice(0, ZS - 1), spent)
            else:
                sends = [(pick(1 - own[axis], own), pick(0, spent))]
                arrived = [pick(0, spent)]
                both = sends[0]
            plan.append((pick(own[axis], own), arrived, sends, targets[axis], both))
        return plan

    def rs_copies(s, phase):
        a, b, parts = REDUCES[s]
        copies, waits = [], []
        if phase == 0:
            cols = pl.ds(parts[0][0], sum(count for _, count, _ in parts))
            every = slice(None)
            src = g_buf.at[pl.ds(a, b - a), every, every, every, 1 - c, every, cols]
            dst = rc.at[pl.ds(a, b - a), every, every, every, every, cols]
            at = AT_REDUCE[s]
            copies.append(remote(src, dst, rs_s.at[at], rs_r.at[at], other_c))
            return copies, copies
        if parts[0][2] == "all":
            m, cols = pl.ds(a, b - a), pl.ds(parts[0][0], parts[0][1])
            for k, (dx, dy, steps) in enumerate(apart):
                at = AT_REDUCE[s] + 1 + k
                for dz, device in steps:
                    kept = rc.at[m, (gi + dx) % 2, (z + dz) % ZS, (y + dy) % 2, :, cols]
                    copies.append(remote(kept, rx.at[m, dx, dz, dy, :, cols], rs_s.at[at], rs_r.at[at], device))
                arrived = rx.at[m, dx, pl.ds(steps[0][0], len(steps)), dy, :, cols]
                waits.append(remote(arrived, arrived, rs_s.at[at], rs_r.at[at], steps[0][1]))
            return copies, waits
        for k, (_, _, sends, devices, both) in enumerate(rs_plan(s, phase)):
            at = AT_REDUCE[s] + 1 + (phase - 1) * len(parts) + k
            for (kept, slot), device in zip(sends, devices):
                copies.append(remote(rc.at[kept], rx.at[slot], rs_s.at[at], rs_r.at[at], device))
            waits.append(remote(rc.at[both[0]], rx.at[both[1]], rs_s.at[at], rs_r.at[at], devices[0]))
        return copies, waits

    def rs_start(s, phase):
        for copy in rs_copies(s, phase)[0]:
            copy.start()

    def rs_wait(s, phase):
        for copy in rs_copies(s, phase)[1]:
            copy.wait()

    def rs_add(s, phase):
        a, b, parts = REDUCES[s]
        for m in range(a, b):
            if phase == 0:
                for first, count, _ in parts:
                    cols = slice(first, first + count)
                    rc[m, :, :, :, :, cols] = rc[m, :, :, :, :, cols] + g_buf[m, :, :, :, c, :, cols]
                continue
            if parts[0][2] == "all":
                cols = slice(parts[0][0], parts[0][0] + parts[0][1])
                total = rc[m, gi, z, y, :, cols].astype(F32)
                for dx, dy, steps in apart:
                    for dz, _ in steps:
                        total = total + rx[m, dx, dz, dy, :, cols].astype(F32)
                grad_ref[m, :, cols] = total
                continue
            for (first, count, order), (own, arrived, _, _, _) in zip(parts, rs_plan(s, phase)):
                own = (m, *own[1:])
                got = [rx[(m, *slot[1:])] for slot in arrived]
                last = phase == len(order.split(","))
                if len(got) == 1 and not last:
                    rc[own] = rc[own] + got[0]
                    continue
                total = rc[own].astype(F32)
                for one in got:
                    total = total + one.astype(F32)
                if last:
                    grad_ref[m, :, first : first + count] = total
                else:
                    rc[own] = total.astype(BF16)

    def rs_step(s, phase):
        if phase:
            rs_wait(s, phase - 1)
            rs_add(s, phase - 1)
        if phase <= len(axes_of(REDUCES[s][2])):
            rs_start(s, phase)

    def vec_copies(phase):
        if phase == 3:
            copies = [
                remote(
                    vec_sum.at[3, pl.ds(0, 4)], vec_got.at[2 + i, pl.ds(0, 4)], vs_s.at[3], vs_r.at[3], others_z[i - 1]
                )
                for i in range(1, ZS)
            ]
            three = vec_got.at[pl.ds(3, ZS - 1), pl.ds(0, 4)]
            return copies, [remote(three, three, vs_s.at[3], vs_r.at[3], others_z[0])]
        device = (other_c, other_y, other_x)[phase]
        rows = pl.ds(0, 4)
        copies = [
            remote(vec_sum.at[phase, rows], vec_got.at[phase, rows], vs_s.at[phase], vs_r.at[phase], device)
        ]
        return copies, copies

    def vec_step(phase):
        if phase:
            for copy in vec_copies(phase - 1)[1]:
                copy.wait()
            if phase < 4:
                vec_sum[phase, 0:4] = vec_sum[phase - 1, 0:4] + vec_got[phase - 1, 0:4]
        if phase < 4:
            for copy in vec_copies(phase)[0]:
                copy.start()

    def local_copy(index, src, dst):
        return pltpu.make_async_copy(src, dst, swap_s.at[index])

    def swap_copy(index, src, dst):
        return remote(src, dst, swap_s.at[index], swap_r.at[index], partner)

    def point(name):
        for step in SCHEDULE.get(name, ()):
            if step == "tokens":
                send_tokens()
            elif step == "cotangent":
                send_cotangent()
            elif step == "result":
                send_result()
            else:
                kind, phase = step.split(".")
                if kind == "vec":
                    vec_step(int(phase))
                else:
                    (ag_step if kind[0] == "g" else rs_step)(int(kind[1:]), int(phase))

    def send_tokens():
        @pl.when(swaps)
        def _():
            swap_copy(0, meta_own, meta).start()
            swap_copy(1, tok_ref, x_in).start()

        @pl.when(jnp.logical_not(swaps))
        def _():
            meta[...] = meta_own[...]
            local_copy(0, tok_ref, x_in).start()
            local_copy(1, cot_ref, cot).start()

    def send_cotangent():
        @pl.when(swaps)
        def _():
            swap_copy(2, cot_ref, cot).start()

    def send_result():
        @pl.when(swaps)
        def _():
            swap_copy(4, cot, inp_ref).start()

        @pl.when(jnp.logical_not(swaps))
        def _():
            local_copy(4, cot, inp_ref).start()

    for l in range(2):
        for row in range(16):
            flat = slice(row * d, (row + 1) * d)
            feeds = ff_ref[l, :, flat].astype(F32)
            rows = {
                KEY: qkv_ref[1, l : l + 1, flat].astype(F32),
                VALUE: qkv_ref[2, l : l + 1, flat].astype(F32),
                QUERY: qkv_ref[0, l : l + 1, flat].astype(F32),
                OUT: outw_ref[l : l + 1, flat].astype(F32), UP: feeds[0:1], DOWN: feeds[1:2],
            }
            for index, value in rows.items():
                at = (l * 6 + index) * 16 + row
                dkk[at : at + 1, :] = value
    for index in range(12):
        w[place_of(index // 6, index % 6), gi, z, y, c] = dkk[index * 16 : index * 16 + 16, :].astype(BF16)
    per = 2 * d // BLOCKS
    dvv[0:16, 0:128] = jnp.zeros((16, 128), F32)
    dvv[0:2, 0:per] = gain_ref[...].astype(F32)
    dvv[2:4, 0:per] = shift_ref[...].astype(F32)
    w[VECTORS, gi, z, y, c, :, 0:128] = dvv[0:16, 0:128].astype(BF16)
    position = order_ref[...]
    cell = jnp.zeros(position.shape, jnp.int32)
    edge = jnp.zeros((1, 1), jnp.int32)
    for i in range(length_ref.shape[1]):
        edge = edge + length_ref[:, i : i + 1]
        cell = cell + (edge <= position).astype(jnp.int32)
    meta_own[0:1, :] = cell.astype(F32)
    meta_own[1:2, 0:n] = known_ref[...].astype(F32)

    pl.semaphore_wait(barrier, len(partners))
    point("start")

    pair_lane = lax.broadcasted_iota(jnp.int32, (HEADS, 128), 1)
    pair_row = lax.broadcasted_iota(jnp.int32, (HEADS, 128), 0)
    head_of = (pair_lane // hd == pair_row).astype(BF16)
    code_at = (pair_lane % hd == pair_row).astype(BF16)
    tall_lane = lax.broadcasted_iota(jnp.int32, (n, 128), 1)
    of_head = (tall_lane < hd, tall_lane >= hd)
    first_lane = tall_lane % hd == 0
    second_lane = tall_lane % hd == 1
    block_row = lax.broadcasted_iota(jnp.int32, (128, 128), 0) // hd
    block_lane = lax.broadcasted_iota(jnp.int32, (128, 128), 1) // hd
    same_head = (block_row == block_lane).astype(BF16)
    other_head = (block_row != block_lane).astype(BF16)

    def two_parts(product):
        high = product.astype(BF16)
        return high, (product - high.astype(F32)).astype(BF16)

    def weight(l, index):
        return w[place_of(l, index)].reshape(d, d)

    @pl.when(swaps)
    def _():
        swap_copy(0, meta_own, meta).wait()

    kinds = lax.broadcasted_iota(jnp.int32, (HEADS, n), 0).astype(F32)
    query_cell = jnp.where(is_known, meta[0:1, 0:n], meta[0:1, n : 2 * n])
    query_kind = (kinds == query_cell).astype(BF16)
    key_kind = ((kinds == meta[0:1, 0:n]) & (meta[1:2, 0:n] == 1.0)).astype(BF16)
    query_code[...] = dot(query_kind, code_at, 0, 0).astype(BF16)
    key_code[...] = jnp.where(
        tall_lane % hd < HEADS, (1.0 - dot(key_kind, code_at, 0, 0)) * -1e30, 0.0
    ).astype(BF16)
    found_self[...] = jnp.where(is_known & (meta[1:2, 0:n] == 1.0), -1e30, 0.0)

    point("coded")

    def receive_tokens():
        @pl.when(swaps)
        def _():
            swap_copy(1, tok_ref, x_in).wait()

        @pl.when(jnp.logical_not(swaps))
        def _():
            local_copy(0, tok_ref, x_in).wait()

        low[0] = x_in[...]
        cur[...] = x_in[...].astype(F32)

    def need(name):
        point(name)
        if name in NEEDS:
            ag_finish(NEEDS[name])

    def in_head(h, value, other=0.0):
        return jnp.where(of_head[h], value, jnp.asarray(other, value.dtype))

    def lanes_of(i):
        if isinstance(i, int):
            return slice(i * 128, i * 128 + 128)
        return pl.ds(pl.multiple_of(i * 128, 128), 128)

    def columns_of(segment):
        return slice(segment[0], sum(segment))

    def kv_copy(l, part):
        block = kkv.at[l, :, :, pl.ds(*SEGMENTS[l][part])]
        at = l * len(SEGMENTS[0]) + part
        return remote(block, block, kv_s.at[at], kv_r.at[at], sibling)

    def for_pairs(segment, step):
        first, last = segment[0] // 128, sum(segment) // 128
        if last - first == 1:
            step(first, first, last)
        else:
            lax.fori_loop(first, last, lambda i, carry: step(i, first, last), None)

    def loop_point(form, i, first, last):
        if last - first == 1:
            need(form % first)
            return
        for k in range(first, last):
            name = form % k
            if name in NEEDS or SCHEDULE.get(name):
                pl.when(i == k)(functools.partial(need, name))

    def own_wide_of(l, i):
        return dot(own_e[l, i].astype(BF16), head_of, 0, 0)

    def project(l, part):
        need(f"layer {l} need {part}")
        if l + part == 0:
            receive_tokens()
        lanes = columns_of(SEGMENTS[l][part])
        start, count = SEGMENTS[l][part]

        def apply(index):
            return dot(low[l], w[place_of(l, index), :, :, :, :, :, lanes].reshape(d, count), 1, 0).astype(BF16)

        ks[l, :, lanes] = apply(KEY)
        vs[l, :, lanes] = apply(VALUE)

        @pl.when(is_known)
        def _():
            kkv[l, 0, :, lanes] = ks[l, :, lanes]
            kkv[l, 1, :, lanes] = vs[l, :, lanes]
            kv_copy(l, part).start()

        qs[l, :, lanes] = (apply(QUERY).astype(F32) * scale).astype(BF16)
        high, rest = two_parts(qs[l, :, lanes].astype(F32) * ks[l, :, lanes].astype(F32))
        for i in range(start // 128, (start + count) // 128):
            here = slice(i * 128 - start, i * 128 - start + 128)
            own = dot(head_of, high[:, here], 1, 1) + dot(head_of, rest[:, here], 1, 1)
            own_e[l, i] = jnp.where(found_self[...] < 0.0, -1e30, own)
        point(f"layer {l} columns {part}")

        @pl.when(jnp.logical_not(is_known))
        def _():
            kv_copy(l, part).wait_recv()

    def attend(l, i, first, last):
        lanes = lanes_of(i)
        q_pair = qs[l, :, lanes]
        own = own_e[l, i]
        k_pair, v_pair = kkv[l, 0, :, lanes], kkv[l, 1, :, lanes]
        codes = query_code[...], key_code[...]
        outs, owns = [], []
        for h in range(2):
            own_score = own[h : h + 1, :]
            scores = dot(
                jnp.where(of_head[h], k_pair, codes[1]), jnp.where(of_head[h], q_pair, codes[0]), 1, 1
            )
            top = jnp.maximum(jnp.max(scores, axis=0, keepdims=True), own_score)
            weights = jnp.exp(scores - top).astype(BF16)
            owns.append(jnp.exp(own_score - top))
            probs[l, i * 2 + h] = weights
            outs.append(dot(weights, in_head(h, v_pair, 1.0), 0, 0))
        own_e[l, i] = jnp.concatenate(owns + [jnp.zeros((HEADS - 2, n), F32)], axis=0)
        own_wide = own_wide_of(l, i)
        inverse = 1.0 / (pltpu.roll(jnp.where(of_head[0], outs[1], outs[0]), hd, 1) + own_wide)
        total = jnp.where(of_head[0], outs[0], outs[1]) + own_wide * vs[l, :, lanes].astype(F32)
        inverses[l, :, lanes] = inverse
        ctx[l, :, lanes] = (total * inverse).astype(BF16)
        loop_point(f"layer {l} pair %d", i, first, last)

    def norm(values, gain, shift, xhat, spread):
        center = values - jnp.mean(values, axis=1, keepdims=True)
        r = lax.rsqrt(jnp.mean(center * center, axis=1, keepdims=True) + 1e-05)
        hat = center * r
        xhat[...] = hat.astype(BF16)
        spread[...] = r
        return hat * gain + shift

    def vectors(l):
        blocks = w[VECTORS, :, :, :, :, :, 0:128].reshape(BLOCKS, 16, 128).astype(F32)
        wide = 2 * d
        source = lax.broadcasted_iota(jnp.int32, (128, wide), 0)
        target = lax.broadcasted_iota(jnp.int32, (128, wide), 1)
        owner = lax.broadcasted_iota(jnp.int32, (BLOCKS, wide), 0)
        column = lax.broadcasted_iota(jnp.int32, (BLOCKS, wide), 1)
        pick = (source == target % per).astype(BF16)
        mine = column // per == owner
        found = []
        for row in (l, 2 + l):
            spread_out = dot(blocks[:, row, :].astype(BF16), pick, 1, 0)
            found.append(jnp.sum(jnp.where(mine, spread_out, 0.0), axis=0, keepdims=True))
        gains, shifts = found
        return gains[:, :d], shifts[:, :d], gains[:, d:], shifts[:, d:]

    def feed_forward(l):
        need(f"layer {l} context")
        need(f"layer {l} vectors")
        gain1, shift1, gain2, shift2 = vectors(l)
        first_in = cur[...] + dot(ctx[l], weight(l, OUT), 1, 0)
        normed = norm(first_in, gain1, shift1, xhat1.at[l], r1.at[l])
        work[...] = normed
        normed_low[l] = normed.astype(BF16)
        need(f"layer {l} normed")
        pre_act = dot(normed_low[l], weight(l, UP), 1, 0)
        pre[l] = pre_act
        hidden[l] = jax.nn.gelu(pre_act).astype(BF16)
        need(f"layer {l} hidden")
        second_in = work[...] + dot(hidden[l], weight(l, DOWN), 1, 0)
        cur[...] = norm(second_in, gain2, shift2, xhat2.at[l], r2.at[l])

    for l in range(2):
        if l:
            low[l] = cur[...].astype(BF16)
        for part, segment in enumerate(SEGMENTS[l]):
            project(l, part)
            for_pairs(segment, functools.partial(attend, l))
        feed_forward(l)
        point(f"layer {l} done")
    x_in[...] = cur[...].astype(BF16)

    @pl.when(swaps)
    def _():
        swap_copy(3, x_in, out_ref).start()
        swap_copy(2, cot_ref, cot).wait()

    @pl.when(jnp.logical_not(swaps))
    def _():
        local_copy(3, x_in, out_ref).start()
        local_copy(1, cot_ref, cot).wait()

    cur[...] = cot[...].astype(F32)

    def norm_back(grad, gain, xhat, spread):
        hat = xhat[...].astype(F32)
        e = grad * gain
        mean_e = jnp.mean(e, axis=1, keepdims=True)
        mean_eh = jnp.mean(e * hat, axis=1, keepdims=True)
        out = spread[...] * (e - mean_e - hat * mean_eh)
        return out, jnp.sum(grad * hat, axis=0, keepdims=True), jnp.sum(grad, axis=0, keepdims=True)

    def dkv_copy(l, i):
        lanes = lanes_of(i)
        at = l * pairs + i
        return remote(send_kv.at[l, :, :, lanes], got_kv.at[l, :, :, lanes], dkv_s.at[at], dkv_r.at[at], sibling)

    def store_grad(index, lanes, value):
        g_buf[index, :, :, :, :, :, lanes] = value.astype(BF16).reshape(*g_buf.shape[1:6], value.shape[1])

    every = slice(0, d)

    def backward(l):
        gbase = l * 6
        gain1, shift1, gain2, shift2 = vectors(l)
        grad_second, grad_gain2, grad_shift2 = norm_back(cur[...], gain2, xhat2.at[l], r2.at[l])
        work[...] = grad_second
        grad_ff = grad_second.astype(BF16)
        store_grad(gbase + DOWN, every, dot(hidden[l], grad_ff, 0, 0))
        point(f"back {l} down")
        grad_hidden = dot(grad_ff, weight(l, DOWN), 1, 1)
        act = pre[l]
        coef = math.sqrt(2.0 / math.pi)
        tanh = jnp.tanh(coef * (act + 0.044715 * act * act * act))
        slope = 0.5 * (1.0 + tanh) + 0.5 * act * (1.0 - tanh * tanh) * coef * (1.0 + 3 * 0.044715 * act * act)
        grad_pre = (grad_hidden * slope).astype(BF16)
        store_grad(gbase + UP, every, dot(normed_low[l], grad_pre, 0, 0))
        point(f"back {l} up")
        grad_normed = work[...] + dot(grad_pre, weight(l, UP), 1, 1)
        point(f"back {l} feed")
        grad_first, grad_gain1, grad_shift1 = norm_back(grad_normed, gain1, xhat1.at[l], r1.at[l])
        cur[...] = grad_first
        grad_branch = grad_first.astype(BF16)
        for row, pair in enumerate(((grad_gain1, grad_gain2), (grad_shift1, grad_shift2))):
            at = l * 2 + row
            vec_sum[0, at : at + 1, 0:d] = pair[0]
            vec_sum[0, at : at + 1, d : 2 * d] = pair[1]
        store_grad(gbase + OUT, every, dot(ctx[l], grad_branch, 0, 0))
        point(f"back {l} out")
        dctx[...] = dot(grad_branch, weight(l, OUT), 1, 1).astype(BF16)
        point(f"back {l} context")
        point(f"back {l} attend")
        grad_pairs(l)
        point(f"back {l} wide")
        last_part = len(BACK_SEGMENTS[l]) - 1
        for part, segment in enumerate(BACK_SEGMENTS[l]):
            for_pairs(segment, functools.partial(attend_back, l))
            if part:
                key_grads(l, part - 1)
                point(f"back {l} key {part - 1}")
            query_grads(l, part)
            point(f"back {l} query {part}")
        key_grads(l, last_part)
        point(f"back {l} key {last_part}")
        total = cur[...] + dot(dqb[...], weight(l, QUERY), 1, 1)
        total = total + dot(dkb[...], weight(l, KEY), 1, 1)
        cur[...] = total + dot(dvb[...], weight(l, VALUE), 1, 1)

    def grad_pairs(l):
        for i in range(pairs):
            lanes = slice(i * 128, i * 128 + 128)
            scaled = (dctx[:, lanes].astype(F32) * inverses[l, :, lanes]).astype(BF16)
            dctx[:, lanes] = scaled
            delta = dot(scaled * ctx[l, :, lanes], other_head, 1, 0)
            high, rest = two_parts(delta)
            shifts[:, lanes] = jnp.where(first_lane, -high, jnp.where(second_lane, -rest, jnp.zeros_like(rest)))
            own_grad = dot(scaled * vs[l, :, lanes], same_head, 1, 0)
            own_wide = own_wide_of(l, i)
            own_score = (own_wide * (own_grad - pltpu.roll(delta, hd, 1))).astype(BF16).astype(F32)
            dq[:, lanes] = own_score * ks[l, :, lanes].astype(F32)
            dkk[:, lanes] = own_score * qs[l, :, lanes].astype(F32)
            dvv[:, lanes] = own_wide * scaled.astype(F32)

    def attend_back(l, i, first, last):
        lanes = lanes_of(i)
        k_pair, v_pair, q_pair = kkv[l, 0, :, lanes], kkv[l, 1, :, lanes], qs[l, :, lanes]
        c_pair, shift = dctx[:, lanes], shifts[:, lanes]
        ones = (first_lane | second_lane).astype(BF16)
        sum_q = jnp.zeros((n, 128), F32)
        sum_k = jnp.zeros((n, 128), F32)
        sum_v = jnp.zeros((n, 128), F32)
        for h in range(2):
            prob = probs[l, i * 2 + h]
            grad_prob = dot(
                jnp.where(of_head[h], v_pair, ones), jnp.where(of_head[h], c_pair, shift), 1, 1
            )
            grad_score = (prob.astype(F32) * grad_prob).astype(BF16)
            sum_v = sum_v + dot(prob, in_head(h, c_pair), 1, 0)
            sum_k = sum_k + dot(grad_score, in_head(h, q_pair), 1, 0)
            sum_q = sum_q + dot(grad_score, in_head(h, k_pair), 0, 0)
        dq[:, lanes] += sum_q

        @pl.when(is_known)
        def _():
            dkk[:, lanes] += sum_k
            dvv[:, lanes] += sum_v

        @pl.when(jnp.logical_not(is_known))
        def _():
            send_kv[l, 0, :, lanes] = sum_k.astype(BF16)
            send_kv[l, 1, :, lanes] = sum_v.astype(BF16)
            dkv_copy(l, i).start()

        loop_point(f"back {l} pair %d", i, first, last)

    def query_grads(l, part):
        lanes = columns_of(BACK_SEGMENTS[l][part])
        dqb[:, lanes] = (scale * dq[:, lanes]).astype(BF16)
        store_grad(l * 6 + QUERY, lanes, dot(low[l], dqb[:, lanes], 0, 0))

    def key_grads(l, part):
        lanes = columns_of(BACK_SEGMENTS[l][part])

        @pl.when(is_known)
        def _():
            for i in range(lanes.start // 128, lanes.stop // 128):
                dkv_copy(l, i).wait_recv()
            dkb[:, lanes] = (dkk[:, lanes] + got_kv[l, 0, :, lanes].astype(F32)).astype(BF16)
            dvb[:, lanes] = (dvv[:, lanes] + got_kv[l, 1, :, lanes].astype(F32)).astype(BF16)

        @pl.when(jnp.logical_not(is_known))
        def _():
            dkb[:, lanes] = dkk[:, lanes].astype(BF16)
            dvb[:, lanes] = dvv[:, lanes].astype(BF16)

        store_grad(l * 6 + KEY, lanes, dot(low[l], dkb[:, lanes], 0, 0))
        store_grad(l * 6 + VALUE, lanes, dot(low[l], dvb[:, lanes], 0, 0))

    backward(1)
    backward(0)
    cot[...] = cur[...].astype(BF16)
    point("back 0 done")
    all_sums = vec_sum[3, 0:4]
    for i in range(ZS - 1):
        all_sums = all_sums + vec_got[3 + i, 0:4]
    wide = 2 * d
    me = ((gi * ZS + z) * 2 + y) * 2 + c
    column = lax.broadcasted_iota(jnp.int32, (4, wide), 1)
    mine = jnp.where(column // per == me, all_sums, 0.0)
    source = lax.broadcasted_iota(jnp.int32, (wide, 128), 0)
    target = lax.broadcasted_iota(jnp.int32, (wide, 128), 1)
    fold = (source % per == target).astype(F32)
    vec_ref[0:4, :] = lax.dot_general(
        mine, fold, (((1,), (0,)), ((), ())), preferred_element_type=F32, precision=lax.Precision.HIGHEST
    )
    point("last")

    @pl.when(is_known)
    def _():
        for l in range(2):
            for part in range(len(SEGMENTS[l])):
                kv_copy(l, part).wait_send()

    @pl.when(jnp.logical_not(is_known))
    def _():
        for l in range(2):
            for i in range(pairs):
                dkv_copy(l, i).wait_send()

    @pl.when(swaps)
    def _():
        swap_copy(3, x_in, out_ref).wait()
        swap_copy(4, cot, inp_ref).wait()

    @pl.when(jnp.logical_not(swaps))
    def _():
        local_copy(3, x_in, out_ref).wait()
        local_copy(4, cot, inp_ref).wait()


def run_kernel(replicas, tokens, cotangent, *rest):
    n, d = tokens.shape
    layers = 2
    vmem = pl.BlockSpec(memory_space=pltpu.VMEM)

    def buf(*shape, dtype=BF16):
        return pltpu.VMEM(shape, dtype)

    grid = (2, ZS, 2, 2, 16)
    dma = pltpu.SemaphoreType.DMA
    scratch = [
        buf(MATRICES, *grid, d),
        buf(n, d), buf(n, d),
        buf(8, 2 * n, dtype=F32), buf(8, 2 * n, dtype=F32),
        buf(n, 128), buf(n, 128), buf(1, n, dtype=F32),
        buf(n, d, dtype=F32),
        buf(layers, n, d), buf(layers, n, d), buf(layers, n, d), buf(layers, n, d),
        buf(layers, 2, n, d),
        buf(layers, HEADS, n, n),
        buf(layers, d // 128, HEADS, n, dtype=F32), buf(layers, n, d, dtype=F32),
        buf(layers, n, d),
        buf(layers, n, d), buf(layers, n, 1, dtype=F32),
        buf(layers, n, d), buf(layers, n, d, dtype=F32), buf(layers, n, d),
        buf(layers, n, d), buf(layers, n, 1, dtype=F32),
        buf(n, d, dtype=F32), buf(n, d),
        buf(n, d, dtype=F32), buf(n, d, dtype=F32), buf(n, d, dtype=F32), buf(n, d),
        buf(n, d), buf(n, d), buf(n, d),
        buf(layers, 2, n, d), buf(layers, 2, n, d),
        buf(12, *grid, d),
        buf(12, 2, ZS, 2, 16, d),
        buf(12, 2, ZS, 2, 16, d),
        buf(4, 8, 2 * d, dtype=F32), buf(6, 8, 2 * d, dtype=F32),
        dma((5,)), dma((5,)),
        dma((AT_GATHER[-1],)), dma((AT_GATHER[-1],)),
        dma((6,)), dma((6,)),
        dma((2 * (d // 128),)), dma((2 * (d // 128),)),
        dma((AT_REDUCE[-1],)), dma((AT_REDUCE[-1],)),
        dma((4,)), dma((4,)),
    ]
    return pl.pallas_call(
        functools.partial(kernel, replicas),
        out_shape=(
            jax.ShapeDtypeStruct((n, d), BF16),
            jax.ShapeDtypeStruct((n, d), BF16),
            jax.ShapeDtypeStruct((12, 16, d), F32),
            jax.ShapeDtypeStruct((8, 128), F32),
        ),
        in_specs=[pl.BlockSpec(memory_space=pl.ANY)] * 2 + [vmem] * 8,
        out_specs=(pl.BlockSpec(memory_space=pl.ANY),) * 2 + (vmem,) * 2,
        scratch_shapes=scratch,
        compiler_params=pltpu.CompilerParams(
            collective_id=0, has_side_effects=True, vmem_limit_bytes=62 * 2**20
        ),
    )(tokens, cotangent, *rest)


def finish(
    out_in, inp_in, grad_in, vec_in, layer_out, input_grad, qkv_grad, out_grad, ff_grad, gain_grad, shift_grad,
    low, wide, grad_ref, vec_ref, sems,
):
    d = out_in.shape[1]
    fetch = [
        pltpu.make_async_copy(inp_in, low.at[1], sems.at[0]),
        pltpu.make_async_copy(out_in, low.at[0], sems.at[1]),
        pltpu.make_async_copy(grad_in, grad_ref, sems.at[2]),
        pltpu.make_async_copy(vec_in, vec_ref, sems.at[3]),
    ]
    for copy in fetch:
        copy.start()
    sends = []
    for k, target in ((1, input_grad), (0, layer_out)):
        fetch[1 - k].wait()
        wide[k] = low[k].astype(F32)
        sends.append(pltpu.make_async_copy(wide.at[k], target.at[0], sems.at[4 + k]))
        sends[-1].start()
    fetch[2].wait()
    fetch[3].wait()
    for l in range(2):
        for row in range(16):
            flat = slice(row * d, (row + 1) * d)
            for place, index in enumerate((QUERY, KEY, VALUE)):
                qkv_grad[place, l : l + 1, flat] = grad_ref[l * 6 + index, row : row + 1, :]
            out_grad[l : l + 1, flat] = grad_ref[l * 6 + OUT, row : row + 1, :]
            for place, index in enumerate((UP, DOWN)):
                ff_grad[l, place : place + 1, flat] = grad_ref[l * 6 + index, row : row + 1, :]
    per = gain_grad.shape[1]
    for l in range(2):
        gain_grad[l : l + 1, :] = vec_ref[l * 2 : l * 2 + 1, 0:per]
        shift_grad[l : l + 1, :] = vec_ref[l * 2 + 1 : l * 2 + 2, 0:per]
    for copy in sends:
        copy.wait()


def shards(
    tokens, qkv_weight, out_weight, ff_weight, ln_gain, ln_bias, order, cell_lengths, known_mask, cotangent
):
    _, half_len, d = tokens.shape
    dp_size = lax.axis_size("dp")
    replicas = dp_size * 2 // BLOCKS
    groups = [[i * replicas + j for j in range(replicas)] for i in range(dp_size // replicas)]
    params = [qkv_weight, out_weight, ff_weight, ln_gain, ln_bias]
    if replicas > 1:
        params = [
            lax.all_gather(p, "dp", axis=p.ndim - 1, tiled=True, axis_index_groups=groups) for p in params
        ]
    found = run_kernel(replicas, tokens[0], cotangent[0], jnp.swapaxes(params[0], 0, 1), *params[1:], order, cell_lengths, known_mask)
    vmem = pl.BlockSpec(memory_space=pltpu.VMEM)
    done = list(pl.pallas_call(
        finish,
        out_shape=[jax.ShapeDtypeStruct((1, half_len, d), F32)] * 2
        + [jax.ShapeDtypeStruct((3, 2, params[0].shape[2]), F32)]
        + [jax.ShapeDtypeStruct(p.shape, F32) for p in params[1:]],
        in_specs=[pl.BlockSpec(memory_space=pl.ANY)] * 4,
        out_specs=[pl.BlockSpec(memory_space=pl.ANY)] * 2 + [vmem] * 5,
        scratch_shapes=[
            pltpu.VMEM((2, half_len, d), BF16),
            pltpu.VMEM((2, half_len, d), F32),
            pltpu.VMEM(found[2].shape, F32),
            pltpu.VMEM(found[3].shape, F32),
            pltpu.SemaphoreType.DMA((6,)),
        ],
        compiler_params=pltpu.CompilerParams(vmem_limit_bytes=60 * 2**20),
    )(*found))
    done[2] = jnp.swapaxes(done[2], 0, 1)
    if replicas > 1:
        done[2:] = [
            lax.psum_scatter(g, "dp", scatter_dimension=g.ndim - 1, tiled=True, axis_index_groups=groups)
            for g in done[2:]
        ]
    return tuple(done)


def solution(mesh):
    flat = ("group", "dp")
    return jax.shard_map(
        shards,
        mesh=mesh,
        in_specs=(
            P("dp", "group", None),
            P(None, None, flat),
            P(None, flat),
            P(None, None, flat),
            P(None, flat),
            P(None, flat),
            P("dp", None),
            P("dp", None),
            P("dp", None),
            P("dp", "group", None),
        ),
        out_specs=(
            P("dp", "group", None),
            P("dp", "group", None),
            P(None, None, flat),
            P(None, flat),
            P(None, None, flat),
            P(None, flat),
            P(None, flat),
        ),
        check_vma=False,
    )
```

```python
import functools
import math

import jax
import jax.numpy as jnp
from jax import lax
from jax.experimental import pallas as pl
from jax.experimental.pallas import tpu as pltpu
from jax.sharding import PartitionSpec as P

HEADS = 8
BLOCKS = 32
ZS = 4
MESH = pl.DeviceIdType.MESH
F32 = jnp.float32
BF16 = jnp.bfloat16

KEY, VALUE, QUERY, OUT, UP, DOWN = range(6)
VECTORS = 3
MATRICES = 13
AT_START, AT_CODED, AT_NEED, AT_COLUMNS, AT_PAIR, AT_CONTEXT, AT_VECTORS, AT_NORMED, AT_HIDDEN, AT_DONE = range(10)
BACK_DOWN, BACK_UP, BACK_FEED, BACK_OUT, BACK_CONTEXT, BACK_ATTEND, BACK_WIDE = range(10, 17)
BACK_PAIR, BACK_KEY, BACK_QUERY, BACK_DONE = range(17, 21)
SUM, NORMS, TOKENS, COTANGENT, RESULT = 100, 200, 201, 202, 203
Z_BOTH = "z,both"
BOTH_Z = "both,z"
XYZ = "x,y,z"
XZY = "x,z,y"
YXZ = "y,x,z"
YZX = "y,z,x"
ZXY = "z,x,y"
ZYX = "z,y,x"
GATHERS = (
    (0, 3, ((0, 128, ZYX),)),
    (0, 3, ((128, 128, ZXY),)),
    (0, 3, ((256, 128, XZY), (384, 128, ZYX))),
    (3, 4, ((0, 128, ZYX),)),
    (4, 5, ((0, 256, YZX), (256, 256, ZYX))),
    (5, 6, ((0, 256, ZXY), (256, 256, ZYX))),
    (6, 7, ((0, 256, XZY), (256, 256, ZYX))),
    (7, 10, ((0, 128, YXZ), (128, 128, ZXY))),
    (7, 10, ((256, 128, XYZ), (384, 128, XZY))),
    (10, 11, ((0, 256, ZYX), (256, 256, ZXY))),
    (11, 12, ((0, 512, ZXY),)),
    (12, 13, ((0, 512, YXZ),)),
)
REDUCES = (
    (11, 12, ((0, 512, ZXY),)),
    (10, 11, ((0, 256, XZY), (256, 256, YXZ))),
    (9, 10, ((0, 512, ZXY),)),
    (6, 9, ((0, 128, YZX), (128, 128, ZXY))),
    (6, 9, ((256, 128, XYZ), (384, 128, YXZ))),
    (5, 6, ((0, 256, XYZ), (256, 256, YZX))),
    (4, 5, ((0, 256, YXZ), (256, 256, XYZ))),
    (3, 4, ((0, 256, XYZ), (256, 256, ZXY))),
    (0, 3, ((0, 128, XYZ), (128, 128, YZX))),
    (0, 3, ((256, 128, YZX),)),
    (0, 3, ((384, 128, YXZ),)),
)
SEGMENTS = (((0, 128), (128, 128), (256, 256)), ((0, 256), (256, 256)))
BACK_SEGMENTS = (((0, 256), (256, 128), (384, 128)), ((0, 256), (256, 256)))
NEEDS = {
    (AT_NEED, 0, 0): 0, (AT_NEED, 0, 1): 1, (AT_NEED, 0, 2): 2, (AT_VECTORS, 0, 0): 3, (AT_CONTEXT, 0, 0): 4,
    (AT_NORMED, 0, 0): 5, (AT_HIDDEN, 0, 0): 6, (AT_NEED, 1, 0): 7, (AT_NEED, 1, 1): 8, (AT_CONTEXT, 1, 0): 9,
    (AT_NORMED, 1, 0): 10, (AT_HIDDEN, 1, 0): 11,
}
SCHEDULE = {
    (AT_START, 0, 0): [(0, 0), (1, 0), (2, 0), (4, 0), (3, 0), (TOKENS, 0)],
    (AT_NEED, 0, 0): [(5, 0), (6, 0), (0, 1), (1, 1), (7, 0), (8, 0), (2, 1), (0, 2), (4, 1), (3, 1), (5, 1), (6, 1), (9, 0), (1, 2), (7, 1), (8, 1), (3, 2), (10, 0), (0, 3), (2, 2)],
    (AT_COLUMNS, 0, 0): [(5, 2), (4, 2)],
    (AT_PAIR, 0, 0): [(11, 0), (7, 2), (1, 3), (6, 2), (3, 3)],
    (AT_NEED, 0, 1): [(9, 1)],
    (AT_COLUMNS, 0, 1): [(2, 3)],
    (AT_PAIR, 0, 1): [(5, 3), (8, 2)],
    (AT_COLUMNS, 0, 2): [(11, 1), (10, 1)],
    (AT_PAIR, 0, 2): [(4, 3)],
    (AT_PAIR, 0, 3): [(6, 3)],
    (AT_NORMED, 0, 0): [(9, 2), (7, 3)],
    (AT_HIDDEN, 0, 0): [(11, 2)],
    (AT_DONE, 0, 0): [(COTANGENT, 0)],
    (AT_NEED, 1, 0): [(10, 2)],
    (AT_PAIR, 1, 0): [(8, 3)],
    (AT_PAIR, 1, 1): [(9, 3)],
    (AT_PAIR, 1, 2): [(10, 3)],
    (AT_PAIR, 1, 3): [(11, 3)],
    (BACK_DOWN, 1, 0): [(SUM + 0, 0)],
    (BACK_UP, 1, 0): [(SUM + 1, 0)],
    (BACK_OUT, 1, 0): [(SUM + 2, 0), (SUM + 0, 1)],
    (BACK_WIDE, 1, 0): [(SUM + 1, 1)],
    (BACK_PAIR, 1, 0): [(SUM + 2, 1)],
    (BACK_PAIR, 1, 3): [(SUM + 1, 2)],
    (BACK_KEY, 1, 0): [(SUM + 3, 0)],
    (BACK_QUERY, 1, 1): [(SUM + 0, 2)],
    (BACK_KEY, 1, 1): [(SUM + 4, 0)],
    (BACK_DOWN, 0, 0): [(SUM + 3, 1), (SUM + 5, 0)],
    (BACK_UP, 0, 0): [(SUM + 4, 1), (SUM + 6, 0), (SUM + 0, 3)],
    (BACK_OUT, 0, 0): [(SUM + 7, 0), (SUM + 2, 2), (SUM + 5, 1)],
    (BACK_ATTEND, 0, 0): [(NORMS, 0)],
    (BACK_WIDE, 0, 0): [(SUM + 6, 1), (SUM + 1, 3)],
    (BACK_PAIR, 0, 0): [(NORMS, 1), (SUM + 7, 1)],
    (BACK_PAIR, 0, 1): [(SUM + 4, 2), (SUM + 2, 3)],
    (BACK_QUERY, 0, 0): [(SUM + 0, 4), (SUM + 3, 2)],
    (BACK_PAIR, 0, 2): [(SUM + 5, 2)],
    (BACK_KEY, 0, 0): [(SUM + 8, 0)],
    (BACK_QUERY, 0, 1): [(SUM + 6, 2), (SUM + 1, 4)],
    (BACK_PAIR, 0, 3): [(NORMS, 2), (SUM + 7, 2)],
    (BACK_KEY, 0, 1): [(SUM + 4, 3), (SUM + 9, 0), (SUM + 2, 4), (SUM + 8, 1)],
    (BACK_KEY, 0, 2): [(SUM + 10, 0)],
    (BACK_DONE, 0, 0): [(RESULT, 0), (NORMS, 3), (SUM + 9, 1), (SUM + 6, 3), (SUM + 10, 1), (SUM + 3, 3), (SUM + 7, 3), (SUM + 5, 3), (SUM + 4, 4), (SUM + 8, 2), (NORMS, 4), (SUM + 9, 2), (SUM + 6, 4), (SUM + 10, 2), (SUM + 7, 4), (SUM + 3, 4), (SUM + 5, 4), (SUM + 8, 3), (SUM + 10, 3), (SUM + 9, 3), (SUM + 8, 4), (SUM + 9, 4), (SUM + 10, 4)],
}


def axes_of(parts):
    return parts[0][2].split(",")


def first_semaphores(plan):
    at = [0]
    for _, _, parts in plan:
        at.append(at[-1] + (4 if len(axes_of(parts)) == 2 else 3 * len(parts)) + 1)
    return at


AT_GATHER = first_semaphores(GATHERS)
AT_REDUCE = first_semaphores(REDUCES)


def place_of(l, index):
    return l * 7 + index + (l == 0 and index >= VECTORS)

def dot(left, right, left_dim, right_dim):
    return lax.dot_general(
        left, right, (((left_dim,), (right_dim,)), ((), ())), preferred_element_type=F32
    )


def kernel(replicas, *refs):
    (
        tok_ref, cot_ref, qkv_ref, outw_ref, ff_ref, gain_ref, shift_ref, order_ref, length_ref, known_ref,
        out_ref, inp_ref, grad_ref, vec_ref,
        w, x_in, cot, meta_own, meta, query_code, key_code, found_self, cur, low, qs, ks, vs, kkv, probs, own_e, inverses,
        ctx, xhat1, r1, normed_low, pre, hidden, xhat2, r2, work, dctx, dq, dkk, dvv, shifts, dqb, dkb, dvb,
        send_kv, got_kv,
        g_buf, rc, rx, vec_sum, vec_got,
        swap_s, swap_r, ag_s, ag_r, kv_s, kv_r, dkv_s, dkv_r, rs_s, rs_r, vs_s, vs_r,
    ) = refs
    n, d = tok_ref.shape
    hd = d // HEADS
    pairs = d // 128
    scale = 1.0 / math.sqrt(hd)
    gi = lax.axis_index("group")
    dp = lax.axis_index("dp")
    hi, lo = dp // replicas, dp % replicas
    z, y, c = hi // 4, (hi // 2) % 2, hi % 2
    half = dp % 2

    def place(g_, z_, y_, c_):
        return (g_, (z_ * 4 + y_ * 2 + c_) * replicas + lo)

    other_x = place(1 - gi, z, y, c)
    other_y = place(gi, z, 1 - y, c)
    other_c = place(gi, z, y, 1 - c)
    others_z = [place(gi, (z + i) % ZS, y, c) for i in range(1, ZS)]
    targets = {"x": [other_x], "y": [other_y], "z": others_z}
    apart = [(dx, dy, place((gi + dx) % 2, z, (y + dy) % 2, c)) for dx, dy in ((1, 0), (0, 1), (1, 1))]
    sibling = (gi, dp + 1 - 2 * half)
    partner = (1 - gi, dp + 1 - 2 * half)
    is_known = half == 0
    swaps = gi != half

    partners = [other_c, partner] + others_z + [device for _, _, device in apart]
    if replicas > 1:
        partners.append(sibling)
    barrier = pltpu.get_barrier_semaphore()
    for device in partners:
        pl.semaphore_signal(barrier, inc=1, device_id=device, device_id_type=MESH)

    def remote(src, dst, send, recv, device):
        return pltpu.make_async_remote_copy(
            src_ref=src, dst_ref=dst, send_sem=send, recv_sem=recv, device_id=device, device_id_type=MESH
        )

    def ag_copies(s, phase):
        a, b, parts = GATHERS[s]
        m = pl.ds(a, b - a)
        copies, waits = [], []

        def add(block, three, devices, k):
            at = AT_GATHER[s] + k
            copies.extend(remote(block, block, ag_s.at[at], ag_r.at[at], device) for device in devices)
            waits.append(remote(three, three, ag_s.at[at], ag_r.at[at], devices[0]))

        if phase == len(axes_of(parts)):
            cols = pl.ds(parts[0][0], sum(count for _, count, _ in parts))
            block = w.at[m, :, :, :, c, :, cols]
            add(block, block, [other_c], AT_GATHER[s + 1] - AT_GATHER[s] - 1)
            return copies, waits
        if parts[0][2] == Z_BOTH and phase == 1:
            block = w.at[m, gi, :, y, c, :, pl.ds(parts[0][0], parts[0][1])]
            for k, (_, _, device) in enumerate(apart):
                add(block, block, [device], 1 + k)
            return copies, waits
        for k, (first, count, order) in enumerate(parts):
            axes = order.split(",")
            done = axes[:phase]
            x_at, z_at, y_at = (
                slice(None) if axis in done else own for axis, own in (("x", gi), ("z", z), ("y", y))
            )
            cols = pl.ds(first, count)
            block = w.at[m, x_at, z_at, y_at, c, :, cols]
            three = w.at[m, x_at, pl.ds(0, ZS - 1), y_at, c, :, cols] if axes[phase] == "z" else block
            add(block, three, targets[axes[phase]], phase * len(parts) + k)
        return copies, waits

    def ag_start(s, phase):
        for copy in ag_copies(s, phase)[0]:
            copy.start()

    def ag_wait(s, phase):
        for copy in ag_copies(s, phase)[1]:
            copy.wait()

    def ag_step(s, phase):
        if phase:
            ag_wait(s, phase - 1)
        ag_start(s, phase)

    def ag_finish(s):
        ag_wait(s, len(axes_of(GATHERS[s][2])))

    def rs_plan(s, phase):
        a, b, parts = REDUCES[s]
        m = slice(a, b)
        plan = []
        for first, count, order in parts:
            axes = order.split(",")
            cols = slice(first, first + count)
            axis, before = axes[phase - 1], axes[: phase - 1]

            def pick(value, after):
                where = (value if one == axis else (after[one] if one in before else slice(None)) for one in "xzy")
                return (m, *where, slice(None), cols)

            own = {"x": gi, "y": y, "z": z}
            spent = {"x": 1, "y": 1, "z": ZS - 1}
            if axis == "z":
                sends = [(pick((z + i) % ZS, own), pick(i - 1, spent)) for i in range(1, ZS)]
                arrived = [pick(i, spent) for i in range(ZS - 1)]
                both = pick(slice(0, ZS - 1), own), pick(slice(0, ZS - 1), spent)
            else:
                sends = [(pick(1 - own[axis], own), pick(0, spent))]
                arrived = [pick(0, spent)]
                both = sends[0]
            plan.append((pick(own[axis], own), arrived, sends, targets[axis], both))
        return plan

    def rs_copies(s, phase):
        a, b, parts = REDUCES[s]
        copies, waits = [], []
        if phase == 0:
            cols = pl.ds(parts[0][0], sum(count for _, count, _ in parts))
            every = slice(None)
            src = g_buf.at[pl.ds(a, b - a), every, every, every, 1 - c, every, cols]
            dst = rc.at[pl.ds(a, b - a), every, every, every, every, cols]
            at = AT_REDUCE[s]
            copies.append(remote(src, dst, rs_s.at[at], rs_r.at[at], other_c))
            return copies, copies
        if parts[0][2] == BOTH_Z:
            m, cols = pl.ds(a, b - a), pl.ds(parts[0][0], parts[0][1])
            at = AT_REDUCE[s] + 1
            if phase == 1:
                for k, (dx, dy, device) in enumerate(apart):
                    kept = rc.at[m, (gi + dx) % 2, :, (y + dy) % 2, :, cols]
                    slot = rx.at[m, dx, :, dy, :, cols]
                    copies.append(remote(kept, slot, rs_s.at[at + k], rs_r.at[at + k], device))
                return copies, copies
            for i in range(1, ZS):
                kept, slot = rc.at[m, gi, (z + i) % ZS, y, :, cols], rx.at[m, 0, i - 1, 0, :, cols]
                copies.append(remote(kept, slot, rs_s.at[at + 3], rs_r.at[at + 3], others_z[i - 1]))
            three = rx.at[m, 0, pl.ds(0, ZS - 1), 0, :, cols]
            return copies, [remote(three, three, rs_s.at[at + 3], rs_r.at[at + 3], others_z[0])]
        for k, (_, _, sends, devices, both) in enumerate(rs_plan(s, phase)):
            at = AT_REDUCE[s] + 1 + (phase - 1) * len(parts) + k
            for (kept, slot), device in zip(sends, devices):
                copies.append(remote(rc.at[kept], rx.at[slot], rs_s.at[at], rs_r.at[at], device))
            waits.append(remote(rc.at[both[0]], rx.at[both[1]], rs_s.at[at], rs_r.at[at], devices[0]))
        return copies, waits

    def rs_start(s, phase):
        for copy in rs_copies(s, phase)[0]:
            copy.start()

    def rs_wait(s, phase):
        for copy in rs_copies(s, phase)[1]:
            copy.wait()

    def rs_add(s, phase):
        a, b, parts = REDUCES[s]
        for m in range(a, b):
            if phase == 0:
                for first, count, _ in parts:
                    cols = slice(first, first + count)
                    rc[m, :, :, :, :, cols] = rc[m, :, :, :, :, cols] + g_buf[m, :, :, :, c, :, cols]
                continue
            if parts[0][2] == BOTH_Z:
                cols = slice(parts[0][0], parts[0][0] + parts[0][1])
                if phase == 1:
                    total = rc[m, gi, :, y, :, cols].astype(F32)
                    for dx, dy, _ in apart:
                        total = total + rx[m, dx, :, dy, :, cols].astype(F32)
                    rc[m, gi, :, y, :, cols] = total.astype(BF16)
                else:
                    total = rc[m, gi, z, y, :, cols].astype(F32)
                    for i in range(ZS - 1):
                        total = total + rx[m, 0, i, 0, :, cols].astype(F32)
                    grad_ref[m, :, cols] = total
                continue
            for (first, count, order), (own, arrived, _, _, _) in zip(parts, rs_plan(s, phase)):
                own = (m, *own[1:])
                got = [rx[(m, *slot[1:])] for slot in arrived]
                last = phase == len(order.split(","))
                if len(got) == 1 and not last:
                    rc[own] = rc[own] + got[0]
                    continue
                total = rc[own].astype(F32)
                for one in got:
                    total = total + one.astype(F32)
                if last:
                    grad_ref[m, :, first : first + count] = total
                else:
                    rc[own] = total.astype(BF16)

    def rs_step(s, phase):
        if phase:
            rs_wait(s, phase - 1)
            rs_add(s, phase - 1)
        if phase <= len(axes_of(REDUCES[s][2])):
            rs_start(s, phase)

    def vec_copies(phase):
        if phase == 3:
            copies = [
                remote(
                    vec_sum.at[3, pl.ds(0, 4)], vec_got.at[2 + i, pl.ds(0, 4)], vs_s.at[3], vs_r.at[3], others_z[i - 1]
                )
                for i in range(1, ZS)
            ]
            three = vec_got.at[pl.ds(3, ZS - 1), pl.ds(0, 4)]
            return copies, [remote(three, three, vs_s.at[3], vs_r.at[3], others_z[0])]
        device = (other_c, other_y, other_x)[phase]
        rows = pl.ds(0, 4)
        copies = [
            remote(vec_sum.at[phase, rows], vec_got.at[phase, rows], vs_s.at[phase], vs_r.at[phase], device)
        ]
        return copies, copies

    def vec_step(phase):
        if phase:
            for copy in vec_copies(phase - 1)[1]:
                copy.wait()
            if phase < 4:
                vec_sum[phase, 0:4] = vec_sum[phase - 1, 0:4] + vec_got[phase - 1, 0:4]
        if phase < 4:
            for copy in vec_copies(phase)[0]:
                copy.start()

    def local_copy(index, src, dst):
        return pltpu.make_async_copy(src, dst, swap_s.at[index])

    def swap_copy(index, src, dst):
        return remote(src, dst, swap_s.at[index], swap_r.at[index], partner)

    def point(stage, l, part=0):
        for step, phase in SCHEDULE.get((stage, l, part), ()):
            if step == TOKENS:
                send_tokens()
            elif step == COTANGENT:
                send_cotangent()
            elif step == RESULT:
                send_result()
            elif step == NORMS:
                vec_step(phase)
            elif step >= SUM:
                rs_step(step - SUM, phase)
            else:
                ag_step(step, phase)

    def send_tokens():
        @pl.when(swaps)
        def _():
            swap_copy(0, meta_own, meta).start()
            swap_copy(1, tok_ref, x_in).start()

        @pl.when(jnp.logical_not(swaps))
        def _():
            meta[...] = meta_own[...]
            local_copy(0, tok_ref, x_in).start()
            local_copy(1, cot_ref, cot).start()

    def send_cotangent():
        @pl.when(swaps)
        def _():
            swap_copy(2, cot_ref, cot).start()

    def send_result():
        @pl.when(swaps)
        def _():
            swap_copy(4, cot, inp_ref).start()

        @pl.when(jnp.logical_not(swaps))
        def _():
            local_copy(4, cot, inp_ref).start()

    for l in range(2):
        for row in range(16):
            flat = slice(row * d, (row + 1) * d)
            feeds = ff_ref[l, :, flat].astype(F32)
            rows = {
                KEY: qkv_ref[1, l : l + 1, flat].astype(F32),
                VALUE: qkv_ref[2, l : l + 1, flat].astype(F32),
                QUERY: qkv_ref[0, l : l + 1, flat].astype(F32),
                OUT: outw_ref[l : l + 1, flat].astype(F32), UP: feeds[0:1], DOWN: feeds[1:2],
            }
            for index, value in rows.items():
                at = (l * 6 + index) * 16 + row
                dkk[at : at + 1, :] = value
    for index in range(12):
        w[place_of(index // 6, index % 6), gi, z, y, c] = dkk[index * 16 : index * 16 + 16, :].astype(BF16)
    per = 2 * d // BLOCKS
    dvv[0:16, 0:128] = jnp.zeros((16, 128), F32)
    dvv[0:2, 0:per] = gain_ref[...].astype(F32)
    dvv[2:4, 0:per] = shift_ref[...].astype(F32)
    w[VECTORS, gi, z, y, c, :, 0:128] = dvv[0:16, 0:128].astype(BF16)
    position = order_ref[...]
    cell = jnp.zeros(position.shape, jnp.int32)
    edge = jnp.zeros((1, 1), jnp.int32)
    for i in range(length_ref.shape[1]):
        edge = edge + length_ref[:, i : i + 1]
        cell = cell + (edge <= position).astype(jnp.int32)
    meta_own[0:1, :] = cell.astype(F32)
    meta_own[1:2, 0:n] = known_ref[...].astype(F32)

    pl.semaphore_wait(barrier, len(partners))
    point(AT_START, 0)

    pair_lane = lax.broadcasted_iota(jnp.int32, (HEADS, 128), 1)
    pair_row = lax.broadcasted_iota(jnp.int32, (HEADS, 128), 0)
    head_of = (pair_lane // hd == pair_row).astype(BF16)
    code_at = (pair_lane % hd == pair_row).astype(BF16)
    tall_lane = lax.broadcasted_iota(jnp.int32, (n, 128), 1)
    of_head = (tall_lane < hd, tall_lane >= hd)
    first_lane = tall_lane % hd == 0
    second_lane = tall_lane % hd == 1
    block_row = lax.broadcasted_iota(jnp.int32, (128, 128), 0) // hd
    block_lane = lax.broadcasted_iota(jnp.int32, (128, 128), 1) // hd
    same_head = (block_row == block_lane).astype(BF16)
    other_head = (block_row != block_lane).astype(BF16)

    def two_parts(product):
        high = product.astype(BF16)
        return high, (product - high.astype(F32)).astype(BF16)

    def weight(l, index):
        return w[place_of(l, index)].reshape(d, d)

    @pl.when(swaps)
    def _():
        swap_copy(0, meta_own, meta).wait()

    kinds = lax.broadcasted_iota(jnp.int32, (HEADS, n), 0).astype(F32)
    query_cell = jnp.where(is_known, meta[0:1, 0:n], meta[0:1, n : 2 * n])
    query_kind = (kinds == query_cell).astype(BF16)
    key_kind = ((kinds == meta[0:1, 0:n]) & (meta[1:2, 0:n] == 1.0)).astype(BF16)
    query_code[...] = dot(query_kind, code_at, 0, 0).astype(BF16)
    key_code[...] = jnp.where(
        tall_lane % hd < HEADS, (1.0 - dot(key_kind, code_at, 0, 0)) * -1e30, 0.0
    ).astype(BF16)
    found_self[...] = jnp.where(is_known & (meta[1:2, 0:n] == 1.0), -1e30, 0.0)

    point(AT_CODED, 0)

    def receive_tokens():
        @pl.when(swaps)
        def _():
            swap_copy(1, tok_ref, x_in).wait()

        @pl.when(jnp.logical_not(swaps))
        def _():
            local_copy(0, tok_ref, x_in).wait()

        low[0] = x_in[...]
        cur[...] = x_in[...].astype(F32)

    def need(stage, l, part=0):
        point(stage, l, part)
        if (stage, l, part) in NEEDS:
            ag_finish(NEEDS[stage, l, part])

    def in_head(h, value, other=0.0):
        return jnp.where(of_head[h], value, jnp.asarray(other, value.dtype))

    def lanes_of(i):
        if isinstance(i, int):
            return slice(i * 128, i * 128 + 128)
        return pl.ds(pl.multiple_of(i * 128, 128), 128)

    def columns_of(segment):
        return slice(segment[0], sum(segment))

    def kv_copy(l, part):
        block = kkv.at[l, :, :, pl.ds(*SEGMENTS[l][part])]
        at = l * len(SEGMENTS[0]) + part
        return remote(block, block, kv_s.at[at], kv_r.at[at], sibling)

    def for_pairs(segment, step):
        first, last = segment[0] // 128, sum(segment) // 128
        if last - first == 1:
            step(first, first, last)
        else:
            lax.fori_loop(first, last, lambda i, carry: step(i, first, last), None)

    def loop_point(stage, l, i, first, last):
        if last - first == 1:
            point(stage, l, first)
            return
        for k in range(first, last):
            if SCHEDULE.get((stage, l, k)):
                pl.when(i == k)(functools.partial(point, stage, l, k))

    def own_wide_of(l, i):
        return dot(own_e[l, i].astype(BF16), head_of, 0, 0)

    def project(l, part):
        need(AT_NEED, l, part)
        if l + part == 0:
            receive_tokens()
        lanes = columns_of(SEGMENTS[l][part])
        start, count = SEGMENTS[l][part]

        def apply(index):
            return dot(low[l], w[place_of(l, index), :, :, :, :, :, lanes].reshape(d, count), 1, 0).astype(BF16)

        ks[l, :, lanes] = apply(KEY)
        vs[l, :, lanes] = apply(VALUE)

        @pl.when(is_known)
        def _():
            kkv[l, 0, :, lanes] = ks[l, :, lanes]
            kkv[l, 1, :, lanes] = vs[l, :, lanes]
            kv_copy(l, part).start()

        qs[l, :, lanes] = (apply(QUERY).astype(F32) * scale).astype(BF16)
        high, rest = two_parts(qs[l, :, lanes].astype(F32) * ks[l, :, lanes].astype(F32))
        for i in range(start // 128, (start + count) // 128):
            here = slice(i * 128 - start, i * 128 - start + 128)
            own = dot(head_of, high[:, here], 1, 1) + dot(head_of, rest[:, here], 1, 1)
            own_e[l, i] = jnp.where(found_self[...] < 0.0, -1e30, own)
        point(AT_COLUMNS, l, part)

        @pl.when(jnp.logical_not(is_known))
        def _():
            kv_copy(l, part).wait_recv()

    def attend(l, i, first, last):
        lanes = lanes_of(i)
        q_pair = qs[l, :, lanes]
        own = own_e[l, i]
        k_pair, v_pair = kkv[l, 0, :, lanes], kkv[l, 1, :, lanes]
        codes = query_code[...], key_code[...]
        outs, owns = [], []
        for h in range(2):
            own_score = own[h : h + 1, :]
            scores = dot(
                jnp.where(of_head[h], k_pair, codes[1]), jnp.where(of_head[h], q_pair, codes[0]), 1, 1
            )
            top = jnp.maximum(jnp.max(scores, axis=0, keepdims=True), own_score)
            weights = jnp.exp(scores - top).astype(BF16)
            owns.append(jnp.exp(own_score - top))
            probs[l, i * 2 + h] = weights
            outs.append(dot(weights, in_head(h, v_pair, 1.0), 0, 0))
        own_e[l, i] = jnp.concatenate(owns + [jnp.zeros((HEADS - 2, n), F32)], axis=0)
        own_wide = own_wide_of(l, i)
        inverse = 1.0 / (pltpu.roll(jnp.where(of_head[0], outs[1], outs[0]), hd, 1) + own_wide)
        total = jnp.where(of_head[0], outs[0], outs[1]) + own_wide * vs[l, :, lanes].astype(F32)
        inverses[l, :, lanes] = inverse
        ctx[l, :, lanes] = (total * inverse).astype(BF16)
        loop_point(AT_PAIR, l, i, first, last)

    def norm(values, gain, shift, xhat, spread):
        center = values - jnp.mean(values, axis=1, keepdims=True)
        r = lax.rsqrt(jnp.mean(center * center, axis=1, keepdims=True) + 1e-05)
        hat = center * r
        xhat[...] = hat.astype(BF16)
        spread[...] = r
        return hat * gain + shift

    def vectors(l):
        blocks = w[VECTORS, :, :, :, :, :, 0:128].reshape(BLOCKS, 16, 128).astype(F32)
        wide = 2 * d
        source = lax.broadcasted_iota(jnp.int32, (128, wide), 0)
        target = lax.broadcasted_iota(jnp.int32, (128, wide), 1)
        owner = lax.broadcasted_iota(jnp.int32, (BLOCKS, wide), 0)
        column = lax.broadcasted_iota(jnp.int32, (BLOCKS, wide), 1)
        pick = (source == target % per).astype(BF16)
        mine = column // per == owner
        found = []
        for row in (l, 2 + l):
            spread_out = dot(blocks[:, row, :].astype(BF16), pick, 1, 0)
            found.append(jnp.sum(jnp.where(mine, spread_out, 0.0), axis=0, keepdims=True))
        gains, shifts = found
        return gains[:, :d], shifts[:, :d], gains[:, d:], shifts[:, d:]

    def feed_forward(l):
        need(AT_CONTEXT, l)
        need(AT_VECTORS, l)
        gain1, shift1, gain2, shift2 = vectors(l)
        first_in = cur[...] + dot(ctx[l], weight(l, OUT), 1, 0)
        normed = norm(first_in, gain1, shift1, xhat1.at[l], r1.at[l])
        work[...] = normed
        normed_low[l] = normed.astype(BF16)
        need(AT_NORMED, l)
        pre_act = dot(normed_low[l], weight(l, UP), 1, 0)
        pre[l] = pre_act
        hidden[l] = jax.nn.gelu(pre_act).astype(BF16)
        need(AT_HIDDEN, l)
        second_in = work[...] + dot(hidden[l], weight(l, DOWN), 1, 0)
        cur[...] = norm(second_in, gain2, shift2, xhat2.at[l], r2.at[l])

    for l in range(2):
        if l:
            low[l] = cur[...].astype(BF16)
        for part, segment in enumerate(SEGMENTS[l]):
            project(l, part)
            for_pairs(segment, functools.partial(attend, l))
        feed_forward(l)
        point(AT_DONE, l)
    x_in[...] = cur[...].astype(BF16)

    @pl.when(swaps)
    def _():
        swap_copy(3, x_in, out_ref).start()
        swap_copy(2, cot_ref, cot).wait()

    @pl.when(jnp.logical_not(swaps))
    def _():
        local_copy(3, x_in, out_ref).start()
        local_copy(1, cot_ref, cot).wait()

    cur[...] = cot[...].astype(F32)

    def norm_back(grad, gain, xhat, spread):
        hat = xhat[...].astype(F32)
        e = grad * gain
        mean_e = jnp.mean(e, axis=1, keepdims=True)
        mean_eh = jnp.mean(e * hat, axis=1, keepdims=True)
        out = spread[...] * (e - mean_e - hat * mean_eh)
        return out, jnp.sum(grad * hat, axis=0, keepdims=True), jnp.sum(grad, axis=0, keepdims=True)

    def dkv_copy(l, i):
        lanes = lanes_of(i)
        at = l * pairs + i
        return remote(send_kv.at[l, :, :, lanes], got_kv.at[l, :, :, lanes], dkv_s.at[at], dkv_r.at[at], sibling)

    def store_grad(index, lanes, value):
        g_buf[index, :, :, :, :, :, lanes] = value.astype(BF16).reshape(*g_buf.shape[1:6], value.shape[1])

    every = slice(0, d)

    def backward(l):
        gbase = l * 6
        gain1, shift1, gain2, shift2 = vectors(l)
        grad_second, grad_gain2, grad_shift2 = norm_back(cur[...], gain2, xhat2.at[l], r2.at[l])
        work[...] = grad_second
        grad_ff = grad_second.astype(BF16)
        store_grad(gbase + DOWN, every, dot(hidden[l], grad_ff, 0, 0))
        point(BACK_DOWN, l)
        grad_hidden = dot(grad_ff, weight(l, DOWN), 1, 1)
        act = pre[l]
        coef = math.sqrt(2.0 / math.pi)
        tanh = jnp.tanh(coef * (act + 0.044715 * act * act * act))
        slope = 0.5 * (1.0 + tanh) + 0.5 * act * (1.0 - tanh * tanh) * coef * (1.0 + 3 * 0.044715 * act * act)
        grad_pre = (grad_hidden * slope).astype(BF16)
        store_grad(gbase + UP, every, dot(normed_low[l], grad_pre, 0, 0))
        point(BACK_UP, l)
        grad_normed = work[...] + dot(grad_pre, weight(l, UP), 1, 1)
        point(BACK_FEED, l)
        grad_first, grad_gain1, grad_shift1 = norm_back(grad_normed, gain1, xhat1.at[l], r1.at[l])
        cur[...] = grad_first
        grad_branch = grad_first.astype(BF16)
        for row, pair in enumerate(((grad_gain1, grad_gain2), (grad_shift1, grad_shift2))):
            at = l * 2 + row
            vec_sum[0, at : at + 1, 0:d] = pair[0]
            vec_sum[0, at : at + 1, d : 2 * d] = pair[1]
        store_grad(gbase + OUT, every, dot(ctx[l], grad_branch, 0, 0))
        point(BACK_OUT, l)
        dctx[...] = dot(grad_branch, weight(l, OUT), 1, 1).astype(BF16)
        point(BACK_CONTEXT, l)
        point(BACK_ATTEND, l)
        grad_pairs(l)
        point(BACK_WIDE, l)
        last_part = len(BACK_SEGMENTS[l]) - 1
        for part, segment in enumerate(BACK_SEGMENTS[l]):
            for_pairs(segment, functools.partial(attend_back, l))
            if part:
                key_grads(l, part - 1)
                point(BACK_KEY, l, part - 1)
            query_grads(l, part)
            point(BACK_QUERY, l, part)
        key_grads(l, last_part)
        point(BACK_KEY, l, last_part)
        total = cur[...] + dot(dqb[...], weight(l, QUERY), 1, 1)
        total = total + dot(dkb[...], weight(l, KEY), 1, 1)
        cur[...] = total + dot(dvb[...], weight(l, VALUE), 1, 1)

    def grad_pairs(l):
        for i in range(pairs):
            lanes = slice(i * 128, i * 128 + 128)
            scaled = (dctx[:, lanes].astype(F32) * inverses[l, :, lanes]).astype(BF16)
            dctx[:, lanes] = scaled
            delta = dot(scaled * ctx[l, :, lanes], other_head, 1, 0)
            high, rest = two_parts(delta)
            shifts[:, lanes] = jnp.where(first_lane, -high, jnp.where(second_lane, -rest, jnp.zeros_like(rest)))
            own_grad = dot(scaled * vs[l, :, lanes], same_head, 1, 0)
            own_wide = own_wide_of(l, i)
            own_score = (own_wide * (own_grad - pltpu.roll(delta, hd, 1))).astype(BF16).astype(F32)
            dq[:, lanes] = own_score * ks[l, :, lanes].astype(F32)
            dkk[:, lanes] = own_score * qs[l, :, lanes].astype(F32)
            dvv[:, lanes] = own_wide * scaled.astype(F32)

    def attend_back(l, i, first, last):
        lanes = lanes_of(i)
        k_pair, v_pair, q_pair = kkv[l, 0, :, lanes], kkv[l, 1, :, lanes], qs[l, :, lanes]
        c_pair, shift = dctx[:, lanes], shifts[:, lanes]
        ones = (first_lane | second_lane).astype(BF16)
        sum_q = jnp.zeros((n, 128), F32)
        sum_k = jnp.zeros((n, 128), F32)
        sum_v = jnp.zeros((n, 128), F32)
        for h in range(2):
            prob = probs[l, i * 2 + h]
            grad_prob = dot(
                jnp.where(of_head[h], v_pair, ones), jnp.where(of_head[h], c_pair, shift), 1, 1
            )
            grad_score = (prob.astype(F32) * grad_prob).astype(BF16)
            sum_v = sum_v + dot(prob, in_head(h, c_pair), 1, 0)
            sum_k = sum_k + dot(grad_score, in_head(h, q_pair), 1, 0)
            sum_q = sum_q + dot(grad_score, in_head(h, k_pair), 0, 0)
        dq[:, lanes] += sum_q

        @pl.when(is_known)
        def _():
            dkk[:, lanes] += sum_k
            dvv[:, lanes] += sum_v

        @pl.when(jnp.logical_not(is_known))
        def _():
            send_kv[l, 0, :, lanes] = sum_k.astype(BF16)
            send_kv[l, 1, :, lanes] = sum_v.astype(BF16)
            dkv_copy(l, i).start()

        loop_point(BACK_PAIR, l, i, first, last)

    def query_grads(l, part):
        lanes = columns_of(BACK_SEGMENTS[l][part])
        dqb[:, lanes] = (scale * dq[:, lanes]).astype(BF16)
        store_grad(l * 6 + QUERY, lanes, dot(low[l], dqb[:, lanes], 0, 0))

    def key_grads(l, part):
        lanes = columns_of(BACK_SEGMENTS[l][part])

        @pl.when(is_known)
        def _():
            for i in range(lanes.start // 128, lanes.stop // 128):
                dkv_copy(l, i).wait_recv()
            dkb[:, lanes] = (dkk[:, lanes] + got_kv[l, 0, :, lanes].astype(F32)).astype(BF16)
            dvb[:, lanes] = (dvv[:, lanes] + got_kv[l, 1, :, lanes].astype(F32)).astype(BF16)

        @pl.when(jnp.logical_not(is_known))
        def _():
            dkb[:, lanes] = dkk[:, lanes].astype(BF16)
            dvb[:, lanes] = dvv[:, lanes].astype(BF16)

        store_grad(l * 6 + KEY, lanes, dot(low[l], dkb[:, lanes], 0, 0))
        store_grad(l * 6 + VALUE, lanes, dot(low[l], dvb[:, lanes], 0, 0))

    backward(1)
    backward(0)
    cot[...] = cur[...].astype(BF16)
    point(BACK_DONE, 0)
    all_sums = vec_sum[3, 0:4]
    for i in range(ZS - 1):
        all_sums = all_sums + vec_got[3 + i, 0:4]
    wide = 2 * d
    me = ((gi * ZS + z) * 2 + y) * 2 + c
    column = lax.broadcasted_iota(jnp.int32, (4, wide), 1)
    mine = jnp.where(column // per == me, all_sums, 0.0)
    source = lax.broadcasted_iota(jnp.int32, (wide, 128), 0)
    target = lax.broadcasted_iota(jnp.int32, (wide, 128), 1)
    fold = (source % per == target).astype(F32)
    vec_ref[0:4, :] = lax.dot_general(
        mine, fold, (((1,), (0,)), ((), ())), preferred_element_type=F32, precision=lax.Precision.HIGHEST
    )

    @pl.when(is_known)
    def _():
        for l in range(2):
            for part in range(len(SEGMENTS[l])):
                kv_copy(l, part).wait_send()

    @pl.when(jnp.logical_not(is_known))
    def _():
        for l in range(2):
            for i in range(pairs):
                dkv_copy(l, i).wait_send()

    @pl.when(swaps)
    def _():
        swap_copy(3, x_in, out_ref).wait()
        swap_copy(4, cot, inp_ref).wait()

    @pl.when(jnp.logical_not(swaps))
    def _():
        local_copy(3, x_in, out_ref).wait()
        local_copy(4, cot, inp_ref).wait()


def run_kernel(replicas, tokens, cotangent, *rest):
    n, d = tokens.shape
    layers = 2
    vmem = pl.BlockSpec(memory_space=pltpu.VMEM)

    def buf(*shape, dtype=BF16):
        return pltpu.VMEM(shape, dtype)

    grid = (2, ZS, 2, 2, 16)
    dma = pltpu.SemaphoreType.DMA
    scratch = [
        buf(MATRICES, *grid, d),
        buf(n, d), buf(n, d),
        buf(8, 2 * n, dtype=F32), buf(8, 2 * n, dtype=F32),
        buf(n, 128), buf(n, 128), buf(1, n, dtype=F32),
        buf(n, d, dtype=F32),
        buf(layers, n, d), buf(layers, n, d), buf(layers, n, d), buf(layers, n, d),
        buf(layers, 2, n, d),
        buf(layers, HEADS, n, n),
        buf(layers, d // 128, HEADS, n, dtype=F32), buf(layers, n, d, dtype=F32),
        buf(layers, n, d),
        buf(layers, n, d), buf(layers, n, 1, dtype=F32),
        buf(layers, n, d), buf(layers, n, d, dtype=F32), buf(layers, n, d),
        buf(layers, n, d), buf(layers, n, 1, dtype=F32),
        buf(n, d, dtype=F32), buf(n, d),
        buf(n, d, dtype=F32), buf(n, d, dtype=F32), buf(n, d, dtype=F32), buf(n, d),
        buf(n, d), buf(n, d), buf(n, d),
        buf(layers, 2, n, d), buf(layers, 2, n, d),
        buf(12, *grid, d),
        buf(12, 2, ZS, 2, 16, d),
        buf(12, 2, ZS, 2, 16, d),
        buf(4, 8, 2 * d, dtype=F32), buf(6, 8, 2 * d, dtype=F32),
        dma((5,)), dma((5,)),
        dma((AT_GATHER[-1],)), dma((AT_GATHER[-1],)),
        dma((6,)), dma((6,)),
        dma((2 * (d // 128),)), dma((2 * (d // 128),)),
        dma((AT_REDUCE[-1],)), dma((AT_REDUCE[-1],)),
        dma((4,)), dma((4,)),
    ]
    return pl.pallas_call(
        functools.partial(kernel, replicas),
        out_shape=(
            jax.ShapeDtypeStruct((n, d), BF16),
            jax.ShapeDtypeStruct((n, d), BF16),
            jax.ShapeDtypeStruct((12, 16, d), F32),
            jax.ShapeDtypeStruct((8, 128), F32),
        ),
        in_specs=[pl.BlockSpec(memory_space=pl.ANY)] * 2 + [vmem] * 8,
        out_specs=(pl.BlockSpec(memory_space=pl.ANY),) * 2 + (vmem,) * 2,
        scratch_shapes=scratch,
        compiler_params=pltpu.CompilerParams(
            collective_id=0, has_side_effects=True, vmem_limit_bytes=62 * 2**20
        ),
    )(tokens, cotangent, *rest)


def finish(
    out_in, inp_in, grad_in, vec_in, layer_out, input_grad, qkv_grad, out_grad, ff_grad, gain_grad, shift_grad,
    low, wide, grad_ref, vec_ref, sems,
):
    d = out_in.shape[1]
    fetch = [
        pltpu.make_async_copy(inp_in, low.at[1], sems.at[0]),
        pltpu.make_async_copy(out_in, low.at[0], sems.at[1]),
        pltpu.make_async_copy(grad_in, grad_ref, sems.at[2]),
        pltpu.make_async_copy(vec_in, vec_ref, sems.at[3]),
    ]
    for copy in fetch:
        copy.start()
    sends = []
    for k, target in ((1, input_grad), (0, layer_out)):
        fetch[1 - k].wait()
        wide[k] = low[k].astype(F32)
        sends.append(pltpu.make_async_copy(wide.at[k], target.at[0], sems.at[4 + k]))
        sends[-1].start()
    fetch[2].wait()
    fetch[3].wait()
    for l in range(2):
        for row in range(16):
            flat = slice(row * d, (row + 1) * d)
            for place, index in enumerate((QUERY, KEY, VALUE)):
                qkv_grad[place, l : l + 1, flat] = grad_ref[l * 6 + index, row : row + 1, :]
            out_grad[l : l + 1, flat] = grad_ref[l * 6 + OUT, row : row + 1, :]
            for place, index in enumerate((UP, DOWN)):
                ff_grad[l, place : place + 1, flat] = grad_ref[l * 6 + index, row : row + 1, :]
    per = gain_grad.shape[1]
    for l in range(2):
        gain_grad[l : l + 1, :] = vec_ref[l * 2 : l * 2 + 1, 0:per]
        shift_grad[l : l + 1, :] = vec_ref[l * 2 + 1 : l * 2 + 2, 0:per]
    for copy in sends:
        copy.wait()


def shards(
    tokens, qkv_weight, out_weight, ff_weight, ln_gain, ln_bias, order, cell_lengths, known_mask, cotangent
):
    _, half_len, d = tokens.shape
    dp_size = lax.axis_size("dp")
    replicas = dp_size * 2 // BLOCKS
    groups = [[i * replicas + j for j in range(replicas)] for i in range(dp_size // replicas)]
    params = [qkv_weight, out_weight, ff_weight, ln_gain, ln_bias]
    if replicas > 1:
        params = [
            lax.all_gather(p, "dp", axis=p.ndim - 1, tiled=True, axis_index_groups=groups) for p in params
        ]
    found = run_kernel(replicas, tokens[0], cotangent[0], jnp.swapaxes(params[0], 0, 1), *params[1:], order, cell_lengths, known_mask)
    vmem = pl.BlockSpec(memory_space=pltpu.VMEM)
    done = list(pl.pallas_call(
        finish,
        out_shape=[jax.ShapeDtypeStruct((1, half_len, d), F32)] * 2
        + [jax.ShapeDtypeStruct((3, 2, params[0].shape[2]), F32)]
        + [jax.ShapeDtypeStruct(p.shape, F32) for p in params[1:]],
        in_specs=[pl.BlockSpec(memory_space=pl.ANY)] * 4,
        out_specs=[pl.BlockSpec(memory_space=pl.ANY)] * 2 + [vmem] * 5,
        scratch_shapes=[
            pltpu.VMEM((2, half_len, d), BF16),
            pltpu.VMEM((2, half_len, d), F32),
            pltpu.VMEM(found[2].shape, F32),
            pltpu.VMEM(found[3].shape, F32),
            pltpu.SemaphoreType.DMA((6,)),
        ],
        compiler_params=pltpu.CompilerParams(vmem_limit_bytes=60 * 2**20),
    )(*found))
    done[2] = jnp.swapaxes(done[2], 0, 1)
    if replicas > 1:
        done[2:] = [
            lax.psum_scatter(g, "dp", scatter_dimension=g.ndim - 1, tiled=True, axis_index_groups=groups)
            for g in done[2:]
        ]
    return tuple(done)


def solution(mesh):
    flat = ("group", "dp")
    return jax.shard_map(
        shards,
        mesh=mesh,
        in_specs=(
            P("dp", "group", None),
            P(None, None, flat),
            P(None, flat),
            P(None, None, flat),
            P(None, flat),
            P(None, flat),
            P("dp", None),
            P("dp", None),
            P("dp", None),
            P("dp", "group", None),
        ),
        out_specs=(
            P("dp", "group", None),
            P("dp", "group", None),
            P(None, None, flat),
            P(None, flat),
            P(None, None, flat),
            P(None, flat),
            P(None, flat),
        ),
        check_vma=False,
    )
```

```python
import functools
import math

import jax
import jax.numpy as jnp
from jax import lax
from jax.experimental import pallas as pl
from jax.experimental.pallas import tpu as pltpu
from jax.sharding import PartitionSpec as P

HEADS = 8
BLOCKS = 32
ZS = 4
MESH = pl.DeviceIdType.MESH
F32 = jnp.float32
BF16 = jnp.bfloat16

KEY, VALUE, QUERY, OUT, UP, DOWN = range(6)
VECTORS = 3
MATRICES = 13
AT_START, AT_CODED, AT_NEED, AT_COLUMNS, AT_PAIR, AT_CONTEXT, AT_VECTORS, AT_NORMED, AT_HIDDEN, AT_DONE = range(10)
BACK_DOWN, BACK_UP, BACK_FEED, BACK_OUT, BACK_CONTEXT, BACK_ATTEND, BACK_WIDE = range(10, 17)
BACK_PAIR, BACK_KEY, BACK_QUERY, BACK_DONE = range(17, 21)
SUM, NORMS, TOKENS, COTANGENT, RESULT = 100, 200, 201, 202, 203
Z_BOTH = "z,both"
BOTH_Z = "both,z"
XYZ = "x,y,z"
XZY = "x,z,y"
YXZ = "y,x,z"
YZX = "y,z,x"
ZXY = "z,x,y"
ZYX = "z,y,x"
GATHERS = (
    (0, 3, ((0, 128, ZYX),)),
    (0, 3, ((128, 128, ZYX),)),
    (0, 3, ((256, 128, ZYX), (384, 128, XZY))),
    (3, 4, ((0, 128, XYZ),)),
    (4, 5, ((0, 256, ZYX), (256, 256, ZXY))),
    (5, 6, ((0, 256, XZY), (256, 256, ZYX))),
    (6, 7, ((0, 256, ZYX), (256, 256, XYZ))),
    (7, 10, ((0, 128, XZY), (128, 128, ZYX))),
    (7, 10, ((256, 128, ZYX), (384, 128, YXZ))),
    (10, 11, ((0, 512, ZXY),)),
    (11, 12, ((0, 256, XZY), (256, 256, ZYX))),
    (12, 13, ((0, 512, XYZ),)),
)
REDUCES = (
    (11, 12, ((0, 512, YXZ),)),
    (10, 11, ((0, 512, ZXY),)),
    (9, 10, ((0, 512, ZXY),)),
    (6, 9, ((0, 128, YXZ), (128, 128, XYZ))),
    (6, 9, ((256, 128, YZX), (384, 128, XYZ))),
    (5, 6, ((0, 256, ZYX), (256, 256, XYZ))),
    (4, 5, ((0, 256, ZXY), (256, 256, YXZ))),
    (3, 4, ((0, 256, YXZ), (256, 256, XYZ))),
    (0, 3, ((0, 256, YXZ),)),
    (0, 3, ((256, 128, ZXY), (384, 128, YZX))),
)
SEGMENTS = (((0, 256), (256, 256)), ((0, 256), (256, 256)))
BACK_SEGMENTS = SEGMENTS
NEEDS = {
    (AT_NEED, 0, 0): (0, 1), (AT_NEED, 0, 1): (2,), (AT_VECTORS, 0, 0): (3,), (AT_CONTEXT, 0, 0): (4,),
    (AT_NORMED, 0, 0): (5,), (AT_HIDDEN, 0, 0): (6,), (AT_NEED, 1, 0): (7,), (AT_NEED, 1, 1): (8,),
    (AT_CONTEXT, 1, 0): (9,), (AT_NORMED, 1, 0): (10,), (AT_HIDDEN, 1, 0): (11,),
}
SCHEDULE = {
    (AT_START, 0, 0): [(0, 0), (1, 0), (2, 0), (TOKENS, 0)],
    (AT_NEED, 0, 0): [(5, 0), (4, 0), (0, 1), (3, 0), (7, 0), (1, 1), (6, 0), (2, 1), (0, 2), (8, 0), (4, 1), (5, 1), (3, 1), (1, 2), (7, 1), (11, 0), (9, 0), (10, 0), (6, 1), (0, 3), (2, 2), (4, 2), (8, 1), (3, 2), (1, 3), (5, 2)],
    (AT_COLUMNS, 0, 0): [(11, 1), (6, 2)],
    (AT_PAIR, 0, 0): [(7, 2), (2, 3)],
    (AT_PAIR, 0, 1): [(9, 1), (4, 3), (10, 1)],
    (AT_COLUMNS, 0, 1): [(3, 3), (8, 2)],
    (AT_PAIR, 0, 2): [(5, 3), (11, 2)],
    (AT_PAIR, 0, 3): [(6, 3)],
    (AT_NORMED, 0, 0): [(7, 3)],
    (AT_HIDDEN, 0, 0): [(10, 2)],
    (AT_DONE, 0, 0): [(9, 2), (COTANGENT, 0)],
    (AT_PAIR, 1, 0): [(8, 3)],
    (AT_PAIR, 1, 1): [(10, 3)],
    (AT_PAIR, 1, 2): [(9, 3)],
    (AT_PAIR, 1, 3): [(11, 3)],
    (BACK_DOWN, 1, 0): [(SUM + 0, 0)],
    (BACK_UP, 1, 0): [(SUM + 1, 0)],
    (BACK_OUT, 1, 0): [(SUM + 0, 1), (SUM + 2, 0)],
    (BACK_WIDE, 1, 0): [(SUM + 1, 1)],
    (BACK_PAIR, 1, 0): [(SUM + 2, 1)],
    (BACK_PAIR, 1, 2): [(SUM + 0, 2)],
    (BACK_KEY, 1, 0): [(SUM + 3, 0)],
    (BACK_KEY, 1, 1): [(SUM + 4, 0)],
    (BACK_DOWN, 0, 0): [(SUM + 3, 1), (SUM + 5, 0), (SUM + 0, 3), (SUM + 1, 2)],
    (BACK_UP, 0, 0): [(SUM + 6, 0), (SUM + 4, 1)],
    (BACK_OUT, 0, 0): [(SUM + 5, 1), (SUM + 7, 0)],
    (BACK_ATTEND, 0, 0): [(NORMS, 0)],
    (BACK_WIDE, 0, 0): [(SUM + 2, 2), (SUM + 6, 1)],
    (BACK_PAIR, 0, 0): [(NORMS, 1), (SUM + 3, 2), (SUM + 7, 1), (SUM + 0, 4), (SUM + 1, 3)],
    (BACK_QUERY, 0, 0): [(SUM + 4, 2)],
    (BACK_PAIR, 0, 2): [(NORMS, 2), (SUM + 5, 2)],
    (BACK_PAIR, 0, 3): [(SUM + 3, 3), (SUM + 2, 3)],
    (BACK_KEY, 0, 0): [(SUM + 8, 0), (SUM + 6, 2)],
    (BACK_QUERY, 0, 1): [(SUM + 1, 4)],
    (BACK_KEY, 0, 1): [(SUM + 9, 0), (NORMS, 3), (SUM + 7, 2)],
    (BACK_DONE, 0, 0): [(RESULT, 0), (SUM + 8, 1), (SUM + 5, 3), (SUM + 2, 4), (SUM + 4, 3), (SUM + 9, 1), (SUM + 6, 3), (SUM + 3, 4), (SUM + 7, 3), (NORMS, 4), (SUM + 8, 2), (SUM + 5, 4), (SUM + 4, 4), (SUM + 9, 2), (SUM + 6, 4), (SUM + 7, 4), (SUM + 8, 3), (SUM + 9, 3), (SUM + 8, 4), (SUM + 9, 4)],
}


def axes_of(parts):
    return parts[0][2].split(",")


def first_semaphores(plan):
    at = [0]
    for _, _, parts in plan:
        at.append(at[-1] + (4 if len(axes_of(parts)) == 2 else 3 * len(parts)) + 1)
    return at


AT_GATHER = first_semaphores(GATHERS)
AT_REDUCE = first_semaphores(REDUCES)


def place_of(l, index):
    return l * 7 + index + (l == 0 and index >= VECTORS)

def dot(left, right, left_dim, right_dim):
    return lax.dot_general(
        left, right, (((left_dim,), (right_dim,)), ((), ())), preferred_element_type=F32
    )


def kernel(replicas, *refs):
    (
        tok_ref, cot_ref, qkv_ref, outw_ref, ff_ref, gain_ref, shift_ref, order_ref, length_ref, known_ref,
        out_ref, inp_ref, grad_ref, vec_ref,
        w, x_in, cot, meta_own, meta, query_code, key_code, found_self, cur, low, qs, ks, vs, kkv, probs, own_e, inverses, norms,
        ctx, xhat1, r1, normed_low, pre, hidden, xhat2, r2, work, dctx, dq, dkk, dvv, shifts, dqb, dkb, dvb,
        send_kv, got_kv,
        g_buf, rc, rx, vec_sum, vec_got,
        swap_s, swap_r, ag_s, ag_r, kv_s, kv_r, dkv_s, dkv_r, rs_s, rs_r, vs_s, vs_r,
    ) = refs
    n, d = tok_ref.shape
    hd = d // HEADS
    pairs = d // 128
    scale = 1.0 / math.sqrt(hd)
    gi = lax.axis_index("group")
    dp = lax.axis_index("dp")
    hi, lo = dp // replicas, dp % replicas
    z, y, c = hi // 4, (hi // 2) % 2, hi % 2
    half = dp % 2

    def place(g_, z_, y_, c_):
        return (g_, (z_ * 4 + y_ * 2 + c_) * replicas + lo)

    other_x = place(1 - gi, z, y, c)
    other_y = place(gi, z, 1 - y, c)
    other_c = place(gi, z, y, 1 - c)
    others_z = [place(gi, (z + i) % ZS, y, c) for i in range(1, ZS)]
    targets = {"x": [other_x], "y": [other_y], "z": others_z}
    apart = [(dx, dy, place((gi + dx) % 2, z, (y + dy) % 2, c)) for dx, dy in ((1, 0), (0, 1), (1, 1))]
    sibling = (gi, dp + 1 - 2 * half)
    partner = (1 - gi, dp + 1 - 2 * half)
    is_known = half == 0
    swaps = gi != half

    partners = [other_c, partner] + others_z + [device for _, _, device in apart]
    if replicas > 1:
        partners.append(sibling)
    barrier = pltpu.get_barrier_semaphore()
    for device in partners:
        pl.semaphore_signal(barrier, inc=1, device_id=device, device_id_type=MESH)

    def remote(src, dst, send, recv, device):
        return pltpu.make_async_remote_copy(
            src_ref=src, dst_ref=dst, send_sem=send, recv_sem=recv, device_id=device, device_id_type=MESH
        )

    def ag_copies(s, phase):
        a, b, parts = GATHERS[s]
        m = pl.ds(a, b - a)
        copies, waits = [], []

        def add(block, three, devices, k):
            at = AT_GATHER[s] + k
            copies.extend(remote(block, block, ag_s.at[at], ag_r.at[at], device) for device in devices)
            waits.append(remote(three, three, ag_s.at[at], ag_r.at[at], devices[0]))

        if phase == len(axes_of(parts)):
            cols = pl.ds(parts[0][0], sum(count for _, count, _ in parts))
            block = w.at[m, :, :, :, c, :, cols]
            add(block, block, [other_c], AT_GATHER[s + 1] - AT_GATHER[s] - 1)
            return copies, waits
        if parts[0][2] == Z_BOTH and phase == 1:
            block = w.at[m, gi, :, y, c, :, pl.ds(parts[0][0], parts[0][1])]
            for k, (_, _, device) in enumerate(apart):
                add(block, block, [device], 1 + k)
            return copies, waits
        for k, (first, count, order) in enumerate(parts):
            axes = order.split(",")
            done = axes[:phase]
            x_at, z_at, y_at = (
                slice(None) if axis in done else own for axis, own in (("x", gi), ("z", z), ("y", y))
            )
            cols = pl.ds(first, count)
            block = w.at[m, x_at, z_at, y_at, c, :, cols]
            three = w.at[m, x_at, pl.ds(0, ZS - 1), y_at, c, :, cols] if axes[phase] == "z" else block
            add(block, three, targets[axes[phase]], phase * len(parts) + k)
        return copies, waits

    def ag_start(s, phase):
        for copy in ag_copies(s, phase)[0]:
            copy.start()

    def ag_wait(s, phase):
        for copy in ag_copies(s, phase)[1]:
            copy.wait()

    def ag_step(s, phase):
        if phase:
            ag_wait(s, phase - 1)
        ag_start(s, phase)

    def ag_finish(s):
        ag_wait(s, len(axes_of(GATHERS[s][2])))

    def rs_plan(s, phase):
        a, b, parts = REDUCES[s]
        m = slice(a, b)
        plan = []
        for first, count, order in parts:
            axes = order.split(",")
            cols = slice(first, first + count)
            axis, before = axes[phase - 1], axes[: phase - 1]

            def pick(value, after):
                where = (value if one == axis else (after[one] if one in before else slice(None)) for one in "xzy")
                return (m, *where, slice(None), cols)

            own = {"x": gi, "y": y, "z": z}
            spent = {"x": 1, "y": 1, "z": ZS - 1}
            if axis == "z":
                sends = [(pick((z + i) % ZS, own), pick(i - 1, spent)) for i in range(1, ZS)]
                arrived = [pick(i, spent) for i in range(ZS - 1)]
                both = pick(slice(0, ZS - 1), own), pick(slice(0, ZS - 1), spent)
            else:
                sends = [(pick(1 - own[axis], own), pick(0, spent))]
                arrived = [pick(0, spent)]
                both = sends[0]
            plan.append((pick(own[axis], own), arrived, sends, targets[axis], both))
        return plan

    def rs_copies(s, phase):
        a, b, parts = REDUCES[s]
        copies, waits = [], []
        if phase == 0:
            cols = pl.ds(parts[0][0], sum(count for _, count, _ in parts))
            every = slice(None)
            src = g_buf.at[pl.ds(a, b - a), every, every, every, 1 - c, every, cols]
            dst = rc.at[pl.ds(a, b - a), every, every, every, every, cols]
            at = AT_REDUCE[s]
            copies.append(remote(src, dst, rs_s.at[at], rs_r.at[at], other_c))
            return copies, copies
        if parts[0][2] == BOTH_Z:
            m, cols = pl.ds(a, b - a), pl.ds(parts[0][0], parts[0][1])
            at = AT_REDUCE[s] + 1
            if phase == 1:
                for k, (dx, dy, device) in enumerate(apart):
                    kept = rc.at[m, (gi + dx) % 2, :, (y + dy) % 2, :, cols]
                    slot = rx.at[m, dx, :, dy, :, cols]
                    copies.append(remote(kept, slot, rs_s.at[at + k], rs_r.at[at + k], device))
                return copies, copies
            for i in range(1, ZS):
                kept, slot = rc.at[m, gi, (z + i) % ZS, y, :, cols], rx.at[m, 0, i - 1, 0, :, cols]
                copies.append(remote(kept, slot, rs_s.at[at + 3], rs_r.at[at + 3], others_z[i - 1]))
            three = rx.at[m, 0, pl.ds(0, ZS - 1), 0, :, cols]
            return copies, [remote(three, three, rs_s.at[at + 3], rs_r.at[at + 3], others_z[0])]
        for k, (_, _, sends, devices, both) in enumerate(rs_plan(s, phase)):
            at = AT_REDUCE[s] + 1 + (phase - 1) * len(parts) + k
            for (kept, slot), device in zip(sends, devices):
                copies.append(remote(rc.at[kept], rx.at[slot], rs_s.at[at], rs_r.at[at], device))
            waits.append(remote(rc.at[both[0]], rx.at[both[1]], rs_s.at[at], rs_r.at[at], devices[0]))
        return copies, waits

    def rs_start(s, phase):
        for copy in rs_copies(s, phase)[0]:
            copy.start()

    def rs_wait(s, phase):
        for copy in rs_copies(s, phase)[1]:
            copy.wait()

    def rs_add(s, phase):
        a, b, parts = REDUCES[s]
        for m in range(a, b):
            if phase == 0:
                for first, count, _ in parts:
                    cols = slice(first, first + count)
                    rc[m, :, :, :, :, cols] = rc[m, :, :, :, :, cols] + g_buf[m, :, :, :, c, :, cols]
                continue
            if parts[0][2] == BOTH_Z:
                cols = slice(parts[0][0], parts[0][0] + parts[0][1])
                if phase == 1:
                    total = rc[m, gi, :, y, :, cols].astype(F32)
                    for dx, dy, _ in apart:
                        total = total + rx[m, dx, :, dy, :, cols].astype(F32)
                    rc[m, gi, :, y, :, cols] = total.astype(BF16)
                else:
                    total = rc[m, gi, z, y, :, cols].astype(F32)
                    for i in range(ZS - 1):
                        total = total + rx[m, 0, i, 0, :, cols].astype(F32)
                    grad_ref[m, :, cols] = total
                continue
            for (first, count, order), (own, arrived, _, _, _) in zip(parts, rs_plan(s, phase)):
                own = (m, *own[1:])
                got = [rx[(m, *slot[1:])] for slot in arrived]
                last = phase == len(order.split(","))
                if len(got) == 1 and not last:
                    rc[own] = rc[own] + got[0]
                    continue
                total = rc[own].astype(F32)
                for one in got:
                    total = total + one.astype(F32)
                if last:
                    grad_ref[m, :, first : first + count] = total
                else:
                    rc[own] = total.astype(BF16)

    def rs_step(s, phase):
        if phase:
            rs_wait(s, phase - 1)
            rs_add(s, phase - 1)
        if phase <= len(axes_of(REDUCES[s][2])):
            rs_start(s, phase)

    def vec_copies(phase):
        if phase == 3:
            copies = [
                remote(
                    vec_sum.at[3, pl.ds(0, 4)], vec_got.at[2 + i, pl.ds(0, 4)], vs_s.at[3], vs_r.at[3], others_z[i - 1]
                )
                for i in range(1, ZS)
            ]
            three = vec_got.at[pl.ds(3, ZS - 1), pl.ds(0, 4)]
            return copies, [remote(three, three, vs_s.at[3], vs_r.at[3], others_z[0])]
        device = (other_c, other_y, other_x)[phase]
        rows = pl.ds(0, 4)
        copies = [
            remote(vec_sum.at[phase, rows], vec_got.at[phase, rows], vs_s.at[phase], vs_r.at[phase], device)
        ]
        return copies, copies

    def vec_step(phase):
        if phase:
            for copy in vec_copies(phase - 1)[1]:
                copy.wait()
            if phase < 4:
                vec_sum[phase, 0:4] = vec_sum[phase - 1, 0:4] + vec_got[phase - 1, 0:4]
        if phase < 4:
            for copy in vec_copies(phase)[0]:
                copy.start()

    def local_copy(index, src, dst):
        return pltpu.make_async_copy(src, dst, swap_s.at[index])

    def swap_copy(index, src, dst):
        return remote(src, dst, swap_s.at[index], swap_r.at[index], partner)

    def point(stage, l, part=0):
        for step, phase in SCHEDULE.get((stage, l, part), ()):
            if step == TOKENS:
                send_tokens()
            elif step == COTANGENT:
                send_cotangent()
            elif step == RESULT:
                send_result()
            elif step == NORMS:
                vec_step(phase)
            elif step >= SUM:
                rs_step(step - SUM, phase)
            else:
                ag_step(step, phase)

    def send_tokens():
        @pl.when(swaps)
        def _():
            swap_copy(0, meta_own, meta).start()
            swap_copy(1, tok_ref, x_in).start()

        @pl.when(jnp.logical_not(swaps))
        def _():
            meta[...] = meta_own[...]
            local_copy(0, tok_ref, x_in).start()
            local_copy(1, cot_ref, cot).start()

    def send_cotangent():
        @pl.when(swaps)
        def _():
            swap_copy(2, cot_ref, cot).start()

    def send_result():
        @pl.when(swaps)
        def _():
            swap_copy(4, cot, inp_ref).start()

        @pl.when(jnp.logical_not(swaps))
        def _():
            local_copy(4, cot, inp_ref).start()

    for l in range(2):
        for row in range(16):
            flat = slice(row * d, (row + 1) * d)
            feeds = ff_ref[l, :, flat].astype(F32)
            rows = {
                KEY: qkv_ref[1, l : l + 1, flat].astype(F32),
                VALUE: qkv_ref[2, l : l + 1, flat].astype(F32),
                QUERY: qkv_ref[0, l : l + 1, flat].astype(F32),
                OUT: outw_ref[l : l + 1, flat].astype(F32), UP: feeds[0:1], DOWN: feeds[1:2],
            }
            for index, value in rows.items():
                at = (l * 6 + index) * 16 + row
                dkk[at : at + 1, :] = value
    for index in range(12):
        w[place_of(index // 6, index % 6), gi, z, y, c] = dkk[index * 16 : index * 16 + 16, :].astype(BF16)
    per = 2 * d // BLOCKS
    dvv[0:16, 0:128] = jnp.zeros((16, 128), F32)
    dvv[0:2, 0:per] = gain_ref[...].astype(F32)
    dvv[2:4, 0:per] = shift_ref[...].astype(F32)
    w[VECTORS, gi, z, y, c, :, 0:128] = dvv[0:16, 0:128].astype(BF16)
    position = order_ref[...]
    cell = jnp.zeros(position.shape, jnp.int32)
    edge = jnp.zeros((1, 1), jnp.int32)
    for i in range(length_ref.shape[1]):
        edge = edge + length_ref[:, i : i + 1]
        cell = cell + (edge <= position).astype(jnp.int32)
    meta_own[0:1, :] = cell.astype(F32)
    meta_own[1:2, 0:n] = known_ref[...].astype(F32)

    pl.semaphore_wait(barrier, len(partners))
    point(AT_START, 0)

    pair_lane = lax.broadcasted_iota(jnp.int32, (HEADS, 128), 1)
    pair_row = lax.broadcasted_iota(jnp.int32, (HEADS, 128), 0)
    head_of = (pair_lane // hd == pair_row).astype(BF16)
    code_at = (pair_lane % hd == pair_row).astype(BF16)
    tall_lane = lax.broadcasted_iota(jnp.int32, (n, 128), 1)
    of_head = (tall_lane < hd, tall_lane >= hd)
    first_lane = tall_lane % hd == 0
    second_lane = tall_lane % hd == 1
    block_row = lax.broadcasted_iota(jnp.int32, (128, 128), 0) // hd
    block_lane = lax.broadcasted_iota(jnp.int32, (128, 128), 1) // hd
    same_head = (block_row == block_lane).astype(BF16)
    other_head = (block_row != block_lane).astype(BF16)

    def two_parts(product):
        high = product.astype(BF16)
        return high, (product - high.astype(F32)).astype(BF16)

    def weight(l, index):
        return w[place_of(l, index)].reshape(d, d)

    @pl.when(swaps)
    def _():
        swap_copy(0, meta_own, meta).wait()

    kinds = lax.broadcasted_iota(jnp.int32, (HEADS, n), 0).astype(F32)
    query_cell = jnp.where(is_known, meta[0:1, 0:n], meta[0:1, n : 2 * n])
    query_kind = (kinds == query_cell).astype(BF16)
    key_kind = ((kinds == meta[0:1, 0:n]) & (meta[1:2, 0:n] == 1.0)).astype(BF16)
    query_code[...] = dot(query_kind, code_at, 0, 0).astype(BF16)
    key_code[...] = jnp.where(
        tall_lane % hd < HEADS, (1.0 - dot(key_kind, code_at, 0, 0)) * -1e30, 0.0
    ).astype(BF16)
    found_self[...] = jnp.where(is_known & (meta[1:2, 0:n] == 1.0), -1e30, 0.0)

    point(AT_CODED, 0)

    def receive_tokens():
        @pl.when(swaps)
        def _():
            swap_copy(1, tok_ref, x_in).wait()

        @pl.when(jnp.logical_not(swaps))
        def _():
            local_copy(0, tok_ref, x_in).wait()

        low[0] = x_in[...]
        cur[...] = x_in[...].astype(F32)

    def need(stage, l, part=0):
        point(stage, l, part)
        for s in NEEDS.get((stage, l, part), ()):
            ag_finish(s)

    def in_head(h, value, other=0.0):
        return jnp.where(of_head[h], value, jnp.asarray(other, value.dtype))

    def lanes_of(i):
        if isinstance(i, int):
            return slice(i * 128, i * 128 + 128)
        return pl.ds(pl.multiple_of(i * 128, 128), 128)

    def columns_of(segment):
        return slice(segment[0], sum(segment))

    def kv_copy(l, part):
        block = kkv.at[l, :, :, pl.ds(*SEGMENTS[l][part])]
        at = l * len(SEGMENTS[0]) + part
        return remote(block, block, kv_s.at[at], kv_r.at[at], sibling)

    def for_pairs(segment, step):
        first, last = segment[0] // 128, sum(segment) // 128
        if last - first == 1:
            step(first, first, last)
        else:
            lax.fori_loop(first, last, lambda i, carry: step(i, first, last), None)

    def loop_point(stage, l, i, first, last):
        if last - first == 1:
            point(stage, l, first)
            return
        for k in range(first, last):
            if SCHEDULE.get((stage, l, k)):
                pl.when(i == k)(functools.partial(point, stage, l, k))

    def own_wide_of(l, i):
        return dot(own_e[l, i].astype(BF16), head_of, 0, 0)

    def project(l, part):
        need(AT_NEED, l, part)
        if l + part == 0:
            receive_tokens()
        lanes = columns_of(SEGMENTS[l][part])
        start, count = SEGMENTS[l][part]

        def apply(index):
            return dot(low[l], w[place_of(l, index), :, :, :, :, :, lanes].reshape(d, count), 1, 0).astype(BF16)

        ks[l, :, lanes] = apply(KEY)
        vs[l, :, lanes] = apply(VALUE)

        @pl.when(is_known)
        def _():
            kkv[l, 0, :, lanes] = ks[l, :, lanes]
            kkv[l, 1, :, lanes] = vs[l, :, lanes]
            kv_copy(l, part).start()

        qs[l, :, lanes] = (apply(QUERY).astype(F32) * scale).astype(BF16)
        high, rest = two_parts(qs[l, :, lanes].astype(F32) * ks[l, :, lanes].astype(F32))
        for i in range(start // 128, (start + count) // 128):
            here = slice(i * 128 - start, i * 128 - start + 128)
            own = dot(head_of, high[:, here], 1, 1) + dot(head_of, rest[:, here], 1, 1)
            own_e[l, i] = jnp.where(found_self[...] < 0.0, -1e30, own)
        point(AT_COLUMNS, l, part)

        @pl.when(jnp.logical_not(is_known))
        def _():
            kv_copy(l, part).wait_recv()

    def attend(l, i, first, last):
        lanes = lanes_of(i)
        q_pair = qs[l, :, lanes]
        own = own_e[l, i]
        k_pair, v_pair = kkv[l, 0, :, lanes], kkv[l, 1, :, lanes]
        codes = query_code[...], key_code[...]
        outs, owns = [], []
        for h in range(2):
            own_score = own[h : h + 1, :]
            scores = dot(
                jnp.where(of_head[h], k_pair, codes[1]), jnp.where(of_head[h], q_pair, codes[0]), 1, 1
            )
            top = jnp.maximum(jnp.max(scores, axis=0, keepdims=True), own_score)
            weights = jnp.exp(scores - top).astype(BF16)
            owns.append(jnp.exp(own_score - top))
            probs[l, i * 2 + h] = weights
            outs.append(dot(weights, in_head(h, v_pair, 1.0), 0, 0))
        own_e[l, i] = jnp.concatenate(owns + [jnp.zeros((HEADS - 2, n), F32)], axis=0)
        own_wide = own_wide_of(l, i)
        inverse = 1.0 / (pltpu.roll(jnp.where(of_head[0], outs[1], outs[0]), hd, 1) + own_wide)
        total = jnp.where(of_head[0], outs[0], outs[1]) + own_wide * vs[l, :, lanes].astype(F32)
        inverses[l, :, lanes] = inverse
        ctx[l, :, lanes] = (total * inverse).astype(BF16)
        loop_point(AT_PAIR, l, i, first, last)

    def norm(values, gain, shift, xhat, spread):
        center = values - jnp.mean(values, axis=1, keepdims=True)
        r = lax.rsqrt(jnp.mean(center * center, axis=1, keepdims=True) + 1e-05)
        hat = center * r
        xhat[...] = hat.astype(BF16)
        spread[...] = r
        return hat * gain + shift

    def vectors(l):
        blocks = w[VECTORS, :, :, :, :, :, 0:128].reshape(BLOCKS, 16, 128).astype(F32)
        wide = 2 * d
        source = lax.broadcasted_iota(jnp.int32, (128, wide), 0)
        target = lax.broadcasted_iota(jnp.int32, (128, wide), 1)
        owner = lax.broadcasted_iota(jnp.int32, (BLOCKS, wide), 0)
        column = lax.broadcasted_iota(jnp.int32, (BLOCKS, wide), 1)
        pick = (source == target % per).astype(BF16)
        mine = column // per == owner
        found = []
        for row in (l, 2 + l):
            spread_out = dot(blocks[:, row, :].astype(BF16), pick, 1, 0)
            found.append(jnp.sum(jnp.where(mine, spread_out, 0.0), axis=0, keepdims=True))
        norms[l, 0:1], norms[l, 1:2] = found

    def feed_forward(l):
        need(AT_CONTEXT, l)
        need(AT_VECTORS, l)
        vectors(l)
        gain1, gain2 = norms[l, 0:1, 0:d], norms[l, 0:1, d : 2 * d]
        shift1, shift2 = norms[l, 1:2, 0:d], norms[l, 1:2, d : 2 * d]
        first_in = cur[...] + dot(ctx[l], weight(l, OUT), 1, 0)
        normed = norm(first_in, gain1, shift1, xhat1.at[l], r1.at[l])
        work[...] = normed
        normed_low[l] = normed.astype(BF16)
        need(AT_NORMED, l)
        pre_act = dot(normed_low[l], weight(l, UP), 1, 0)
        pre[l] = pre_act
        hidden[l] = jax.nn.gelu(pre_act).astype(BF16)
        need(AT_HIDDEN, l)
        second_in = work[...] + dot(hidden[l], weight(l, DOWN), 1, 0)
        cur[...] = norm(second_in, gain2, shift2, xhat2.at[l], r2.at[l])

    for l in range(2):
        if l:
            low[l] = cur[...].astype(BF16)
        for part, segment in enumerate(SEGMENTS[l]):
            project(l, part)
            for_pairs(segment, functools.partial(attend, l))
        feed_forward(l)
        point(AT_DONE, l)
    x_in[...] = cur[...].astype(BF16)

    @pl.when(swaps)
    def _():
        swap_copy(3, x_in, out_ref).start()
        swap_copy(2, cot_ref, cot).wait()

    @pl.when(jnp.logical_not(swaps))
    def _():
        local_copy(3, x_in, out_ref).start()
        local_copy(1, cot_ref, cot).wait()

    cur[...] = cot[...].astype(F32)

    def norm_back(grad, gain, xhat, spread):
        hat = xhat[...].astype(F32)
        e = grad * gain
        mean_e = jnp.mean(e, axis=1, keepdims=True)
        mean_eh = jnp.mean(e * hat, axis=1, keepdims=True)
        out = spread[...] * (e - mean_e - hat * mean_eh)
        return out, jnp.sum(grad * hat, axis=0, keepdims=True), jnp.sum(grad, axis=0, keepdims=True)

    def dkv_copy(l, i):
        lanes = lanes_of(i)
        at = l * pairs + i
        return remote(send_kv.at[l, :, :, lanes], got_kv.at[l, :, :, lanes], dkv_s.at[at], dkv_r.at[at], sibling)

    def store_grad(index, lanes, value):
        g_buf[index, :, :, :, :, :, lanes] = value.astype(BF16).reshape(*g_buf.shape[1:6], value.shape[1])

    every = slice(0, d)

    def backward(l):
        gbase = l * 6
        gain1, gain2 = norms[l, 0:1, 0:d], norms[l, 0:1, d : 2 * d]
        grad_second, grad_gain2, grad_shift2 = norm_back(cur[...], gain2, xhat2.at[l], r2.at[l])
        work[...] = grad_second
        grad_ff = grad_second.astype(BF16)
        store_grad(gbase + DOWN, every, dot(hidden[l], grad_ff, 0, 0))
        point(BACK_DOWN, l)
        grad_hidden = dot(grad_ff, weight(l, DOWN), 1, 1)
        act = pre[l]
        coef = math.sqrt(2.0 / math.pi)
        tanh = jnp.tanh(coef * (act + 0.044715 * act * act * act))
        slope = 0.5 * (1.0 + tanh) + 0.5 * act * (1.0 - tanh * tanh) * coef * (1.0 + 3 * 0.044715 * act * act)
        grad_pre = (grad_hidden * slope).astype(BF16)
        store_grad(gbase + UP, every, dot(normed_low[l], grad_pre, 0, 0))
        point(BACK_UP, l)
        grad_normed = work[...] + dot(grad_pre, weight(l, UP), 1, 1)
        point(BACK_FEED, l)
        grad_first, grad_gain1, grad_shift1 = norm_back(grad_normed, gain1, xhat1.at[l], r1.at[l])
        cur[...] = grad_first
        grad_branch = grad_first.astype(BF16)
        for row, pair in enumerate(((grad_gain1, grad_gain2), (grad_shift1, grad_shift2))):
            at = l * 2 + row
            vec_sum[0, at : at + 1, 0:d] = pair[0]
            vec_sum[0, at : at + 1, d : 2 * d] = pair[1]
        store_grad(gbase + OUT, every, dot(ctx[l], grad_branch, 0, 0))
        point(BACK_OUT, l)
        dctx[...] = dot(grad_branch, weight(l, OUT), 1, 1).astype(BF16)
        point(BACK_CONTEXT, l)
        point(BACK_ATTEND, l)
        grad_pairs(l)
        point(BACK_WIDE, l)
        last_part = len(BACK_SEGMENTS[l]) - 1
        for part, segment in enumerate(BACK_SEGMENTS[l]):
            for_pairs(segment, functools.partial(attend_back, l))
            if part:
                key_grads(l, part - 1)
                point(BACK_KEY, l, part - 1)
            query_grads(l, part)
            point(BACK_QUERY, l, part)
        key_grads(l, last_part)
        point(BACK_KEY, l, last_part)
        total = cur[...] + dot(dqb[...], weight(l, QUERY), 1, 1)
        total = total + dot(dkb[...], weight(l, KEY), 1, 1)
        cur[...] = total + dot(dvb[...], weight(l, VALUE), 1, 1)

    def grad_pairs(l):
        for i in range(pairs):
            lanes = slice(i * 128, i * 128 + 128)
            scaled = (dctx[:, lanes].astype(F32) * inverses[l, :, lanes]).astype(BF16)
            dctx[:, lanes] = scaled
            delta = dot(scaled * ctx[l, :, lanes], other_head, 1, 0)
            high, rest = two_parts(delta)
            shifts[:, lanes] = jnp.where(first_lane, -high, jnp.where(second_lane, -rest, jnp.zeros_like(rest)))
            own_grad = dot(scaled * vs[l, :, lanes], same_head, 1, 0)
            own_wide = own_wide_of(l, i)
            own_score = (own_wide * (own_grad - pltpu.roll(delta, hd, 1))).astype(BF16).astype(F32)
            dq[:, lanes] = own_score * ks[l, :, lanes].astype(F32)
            dkk[:, lanes] = own_score * qs[l, :, lanes].astype(F32)
            dvv[:, lanes] = own_wide * scaled.astype(F32)

    def attend_back(l, i, first, last):
        lanes = lanes_of(i)
        k_pair, v_pair, q_pair = kkv[l, 0, :, lanes], kkv[l, 1, :, lanes], qs[l, :, lanes]
        c_pair, shift = dctx[:, lanes], shifts[:, lanes]
        ones = (first_lane | second_lane).astype(BF16)
        sum_q = jnp.zeros((n, 128), F32)
        sum_k = jnp.zeros((n, 128), F32)
        sum_v = jnp.zeros((n, 128), F32)
        for h in range(2):
            prob = probs[l, i * 2 + h]
            grad_prob = dot(
                jnp.where(of_head[h], v_pair, ones), jnp.where(of_head[h], c_pair, shift), 1, 1
            )
            grad_score = (prob.astype(F32) * grad_prob).astype(BF16)
            sum_v = sum_v + dot(prob, in_head(h, c_pair), 1, 0)
            sum_k = sum_k + dot(grad_score, in_head(h, q_pair), 1, 0)
            sum_q = sum_q + dot(grad_score, in_head(h, k_pair), 0, 0)
        dq[:, lanes] += sum_q

        @pl.when(is_known)
        def _():
            dkk[:, lanes] += sum_k
            dvv[:, lanes] += sum_v

        @pl.when(jnp.logical_not(is_known))
        def _():
            send_kv[l, 0, :, lanes] = sum_k.astype(BF16)
            send_kv[l, 1, :, lanes] = sum_v.astype(BF16)
            dkv_copy(l, i).start()

        loop_point(BACK_PAIR, l, i, first, last)

    def query_grads(l, part):
        lanes = columns_of(BACK_SEGMENTS[l][part])
        dqb[:, lanes] = (scale * dq[:, lanes]).astype(BF16)
        store_grad(l * 6 + QUERY, lanes, dot(low[l], dqb[:, lanes], 0, 0))

    def key_grads(l, part):
        lanes = columns_of(BACK_SEGMENTS[l][part])

        @pl.when(is_known)
        def _():
            for i in range(lanes.start // 128, lanes.stop // 128):
                dkv_copy(l, i).wait_recv()
            dkb[:, lanes] = (dkk[:, lanes] + got_kv[l, 0, :, lanes].astype(F32)).astype(BF16)
            dvb[:, lanes] = (dvv[:, lanes] + got_kv[l, 1, :, lanes].astype(F32)).astype(BF16)

        @pl.when(jnp.logical_not(is_known))
        def _():
            dkb[:, lanes] = dkk[:, lanes].astype(BF16)
            dvb[:, lanes] = dvv[:, lanes].astype(BF16)

        store_grad(l * 6 + KEY, lanes, dot(low[l], dkb[:, lanes], 0, 0))
        store_grad(l * 6 + VALUE, lanes, dot(low[l], dvb[:, lanes], 0, 0))

    backward(1)
    backward(0)
    cot[...] = cur[...].astype(BF16)
    point(BACK_DONE, 0)
    all_sums = vec_sum[3, 0:4]
    for i in range(ZS - 1):
        all_sums = all_sums + vec_got[3 + i, 0:4]
    wide = 2 * d
    me = ((gi * ZS + z) * 2 + y) * 2 + c
    column = lax.broadcasted_iota(jnp.int32, (4, wide), 1)
    mine = jnp.where(column // per == me, all_sums, 0.0)
    source = lax.broadcasted_iota(jnp.int32, (wide, 128), 0)
    target = lax.broadcasted_iota(jnp.int32, (wide, 128), 1)
    fold = (source % per == target).astype(F32)
    vec_ref[0:4, :] = lax.dot_general(
        mine, fold, (((1,), (0,)), ((), ())), preferred_element_type=F32, precision=lax.Precision.HIGHEST
    )

    @pl.when(is_known)
    def _():
        for l in range(2):
            for part in range(len(SEGMENTS[l])):
                kv_copy(l, part).wait_send()

    @pl.when(jnp.logical_not(is_known))
    def _():
        for l in range(2):
            for i in range(pairs):
                dkv_copy(l, i).wait_send()

    @pl.when(swaps)
    def _():
        swap_copy(3, x_in, out_ref).wait()
        swap_copy(4, cot, inp_ref).wait()

    @pl.when(jnp.logical_not(swaps))
    def _():
        local_copy(3, x_in, out_ref).wait()
        local_copy(4, cot, inp_ref).wait()


def run_kernel(replicas, tokens, cotangent, *rest):
    n, d = tokens.shape
    layers = 2
    vmem = pl.BlockSpec(memory_space=pltpu.VMEM)

    def buf(*shape, dtype=BF16):
        return pltpu.VMEM(shape, dtype)

    grid = (2, ZS, 2, 2, 16)
    dma = pltpu.SemaphoreType.DMA
    scratch = [
        buf(MATRICES, *grid, d),
        buf(n, d), buf(n, d),
        buf(8, 2 * n, dtype=F32), buf(8, 2 * n, dtype=F32),
        buf(n, 128), buf(n, 128), buf(1, n, dtype=F32),
        buf(n, d, dtype=F32),
        buf(layers, n, d), buf(layers, n, d), buf(layers, n, d), buf(layers, n, d),
        buf(layers, 2, n, d),
        buf(layers, HEADS, n, n),
        buf(layers, d // 128, HEADS, n, dtype=F32), buf(layers, n, d, dtype=F32),
        buf(layers, 8, 2 * d, dtype=F32),
        buf(layers, n, d),
        buf(layers, n, d), buf(layers, n, 1, dtype=F32),
        buf(layers, n, d), buf(layers, n, d, dtype=F32), buf(layers, n, d),
        buf(layers, n, d), buf(layers, n, 1, dtype=F32),
        buf(n, d, dtype=F32), buf(n, d),
        buf(n, d, dtype=F32), buf(n, d, dtype=F32), buf(n, d, dtype=F32), buf(n, d),
        buf(n, d), buf(n, d), buf(n, d),
        buf(layers, 2, n, d), buf(layers, 2, n, d),
        buf(12, *grid, d),
        buf(12, 2, ZS, 2, 16, d),
        buf(12, 2, ZS, 2, 16, d),
        buf(4, 8, 2 * d, dtype=F32), buf(6, 8, 2 * d, dtype=F32),
        dma((5,)), dma((5,)),
        dma((AT_GATHER[-1],)), dma((AT_GATHER[-1],)),
        dma((4,)), dma((4,)),
        dma((2 * (d // 128),)), dma((2 * (d // 128),)),
        dma((AT_REDUCE[-1],)), dma((AT_REDUCE[-1],)),
        dma((4,)), dma((4,)),
    ]
    return pl.pallas_call(
        functools.partial(kernel, replicas),
        out_shape=(
            jax.ShapeDtypeStruct((n, d), BF16),
            jax.ShapeDtypeStruct((n, d), BF16),
            jax.ShapeDtypeStruct((12, 16, d), F32),
            jax.ShapeDtypeStruct((8, 128), F32),
        ),
        in_specs=[pl.BlockSpec(memory_space=pl.ANY)] * 2 + [vmem] * 8,
        out_specs=(pl.BlockSpec(memory_space=pl.ANY),) * 2 + (vmem,) * 2,
        scratch_shapes=scratch,
        compiler_params=pltpu.CompilerParams(
            collective_id=0, has_side_effects=True, vmem_limit_bytes=62 * 2**20
        ),
    )(tokens, cotangent, *rest)


def finish(
    out_in, inp_in, grad_in, vec_in, layer_out, input_grad, qkv_grad, out_grad, ff_grad, gain_grad, shift_grad,
    low, wide, grad_ref, vec_ref, sems,
):
    d = out_in.shape[1]
    fetch = [
        pltpu.make_async_copy(inp_in, low.at[1], sems.at[0]),
        pltpu.make_async_copy(out_in, low.at[0], sems.at[1]),
        pltpu.make_async_copy(grad_in, grad_ref, sems.at[2]),
        pltpu.make_async_copy(vec_in, vec_ref, sems.at[3]),
    ]
    for copy in fetch:
        copy.start()
    sends = []
    for k, target in ((1, input_grad), (0, layer_out)):
        fetch[1 - k].wait()
        wide[k] = low[k].astype(F32)
        sends.append(pltpu.make_async_copy(wide.at[k], target.at[0], sems.at[4 + k]))
        sends[-1].start()
    fetch[2].wait()
    fetch[3].wait()
    for l in range(2):
        for row in range(16):
            flat = slice(row * d, (row + 1) * d)
            for place, index in enumerate((QUERY, KEY, VALUE)):
                qkv_grad[place, l : l + 1, flat] = grad_ref[l * 6 + index, row : row + 1, :]
            out_grad[l : l + 1, flat] = grad_ref[l * 6 + OUT, row : row + 1, :]
            for place, index in enumerate((UP, DOWN)):
                ff_grad[l, place : place + 1, flat] = grad_ref[l * 6 + index, row : row + 1, :]
    per = gain_grad.shape[1]
    for l in range(2):
        gain_grad[l : l + 1, :] = vec_ref[l * 2 : l * 2 + 1, 0:per]
        shift_grad[l : l + 1, :] = vec_ref[l * 2 + 1 : l * 2 + 2, 0:per]
    for copy in sends:
        copy.wait()


def shards(
    tokens, qkv_weight, out_weight, ff_weight, ln_gain, ln_bias, order, cell_lengths, known_mask, cotangent
):
    _, half_len, d = tokens.shape
    dp_size = lax.axis_size("dp")
    replicas = dp_size * 2 // BLOCKS
    groups = [[i * replicas + j for j in range(replicas)] for i in range(dp_size // replicas)]
    params = [qkv_weight, out_weight, ff_weight, ln_gain, ln_bias]
    if replicas > 1:
        params = [
            lax.all_gather(p, "dp", axis=p.ndim - 1, tiled=True, axis_index_groups=groups) for p in params
        ]
    found = run_kernel(replicas, tokens[0], cotangent[0], jnp.swapaxes(params[0], 0, 1), *params[1:], order, cell_lengths, known_mask)
    vmem = pl.BlockSpec(memory_space=pltpu.VMEM)
    done = list(pl.pallas_call(
        finish,
        out_shape=[jax.ShapeDtypeStruct((1, half_len, d), F32)] * 2
        + [jax.ShapeDtypeStruct((3, 2, params[0].shape[2]), F32)]
        + [jax.ShapeDtypeStruct(p.shape, F32) for p in params[1:]],
        in_specs=[pl.BlockSpec(memory_space=pl.ANY)] * 4,
        out_specs=[pl.BlockSpec(memory_space=pl.ANY)] * 2 + [vmem] * 5,
        scratch_shapes=[
            pltpu.VMEM((2, half_len, d), BF16),
            pltpu.VMEM((2, half_len, d), F32),
            pltpu.VMEM(found[2].shape, F32),
            pltpu.VMEM(found[3].shape, F32),
            pltpu.SemaphoreType.DMA((6,)),
        ],
        compiler_params=pltpu.CompilerParams(vmem_limit_bytes=60 * 2**20),
    )(*found))
    done[2] = jnp.swapaxes(done[2], 0, 1)
    if replicas > 1:
        done[2:] = [
            lax.psum_scatter(g, "dp", scatter_dimension=g.ndim - 1, tiled=True, axis_index_groups=groups)
            for g in done[2:]
        ]
    return tuple(done)


def solution(mesh):
    flat = ("group", "dp")
    return jax.shard_map(
        shards,
        mesh=mesh,
        in_specs=(
            P("dp", "group", None),
            P(None, None, flat),
            P(None, flat),
            P(None, None, flat),
            P(None, flat),
            P(None, flat),
            P("dp", None),
            P("dp", None),
            P("dp", None),
            P("dp", "group", None),
        ),
        out_specs=(
            P("dp", "group", None),
            P("dp", "group", None),
            P(None, None, flat),
            P(None, flat),
            P(None, None, flat),
            P(None, flat),
            P(None, flat),
        ),
        check_vma=False,
    )
```
